512 devices in a mesh: face: 8 (over z_hi, x), row: 8 (over z_lo, core), col: 8 (over y).
Axes of the slice: x: 4, y: 8, z: 8 (z_hi: 2, z_lo: 4; z = z_hi * 4 + z_lo), core: 2. Of those that a mesh axis runs over, the one named last changes fastest.
Arguments:
- state: bfloat16 [8, 128, 128, 1024], P('face', None, 'row', 'col'), may hold values from -6 to 6
- conv_in: bfloat16 [5, 256, 128], replicated, may hold values from -0.1875 to 0.1875
- bias_in: float32 [256], replicated, may hold values from -3 to 3
- conv_out: bfloat16 [5, 128, 256], replicated, may hold values from -0.125 to 0.125
- bias_out: float32 [128], replicated, may hold values from -3 to 3
- land: int32 [8, 64], P('face'), may hold values from 0 to 1, as said below
- owner: int32 [8, 64], P('face'), may hold values from 0 to 31, as said below
Outputs:
- new_state: bfloat16 [8, 128, 128, 1024], P('face', None, 'row', 'col')
- ocean: bfloat16 [8, 64, 2, 4, 16, 128], P('face', ('row', 'col'))
The draws below stay inside these ranges and needn't reach their ends.
Inputs may be any that keep to these rules, and one draw needn't show every extreme that they name: `land`: in every face the tiles owned by ocean device 0 are wet. `owner`: within a face each value 0 to 31 owns exactly two tiles, so no device owns more than 2 wet tiles, and device 0 of every face owns exactly 2; devices with index 32 or more own none.
All inputs are finite; a program needn't handle non-finite values.
Results may differ from the reference program's by a relative error of at most 0.0034.
Values may be sent and summed in bfloat16 or wider, within the bound.
No kernel may reach another device: no remote copies, remote signals or barrier semaphores. Data moves between devices by JAX's collectives and lax.ppermute only.
A program may use at most 64 MiB of HBM per device.

```python
import jax
import jax.numpy as jnp
import numpy as np
from jax import lax

C = 128
HID = 256
OC = 4
RD = 16
WD = 128
CAP = 2
FACES = 8
TILES = 64
H = 128
W = 1024
N_ROW = 8
N_COL = 8


def ocean_tables(key):
    perm_key = jax.random.fold_in(key, 11)
    wet_key = jax.random.fold_in(key, 12)
    ranking = jax.vmap(lambda sub_key: jax.random.permutation(sub_key, TILES))(jax.random.split(perm_key, FACES))
    ranking = ranking.astype(jnp.int32)
    owners = ranking // 2
    coin = jax.random.randint(wet_key, (FACES, TILES), 0, 3)
    wet_tiles = jnp.where(ranking < 2, 1, jnp.where(coin > 0, 1, 0)).astype(jnp.int32)
    return (owners, wet_tiles)


def draw_land(key, part):
    owners, wet_tiles = ocean_tables(key)
    return (1 - wet_tiles).astype(jnp.int32)


def draw_owner(key, part):
    owners, wet_tiles = ocean_tables(key)
    return owners.astype(jnp.int32)


def block_scale(stream_key, shape, cuts, low, high):
    loudness = 1.0
    for position, blocks in cuts:
        heights = jax.random.uniform(jax.random.fold_in(jax.random.fold_in(stream_key, 6), position), (blocks,), jnp.float32, low / len(cuts), high / len(cuts))
        loudness = loudness * jnp.repeat(jnp.exp(heights), shape[position] // blocks).reshape((-1,) + (1,) * (len(shape) - 1 - position))
    return loudness


def scatter_about(key, shape, scale, most, cuts=(), kind=jnp.bfloat16):
    result = scale * jax.random.normal(key, shape, jnp.float32)
    if cuts:
        result = result * block_scale(key, shape, cuts, -0.22, 0.18)
    return jnp.clip(result, -most, most).astype(kind)


def setup_inputs(seed: int = 0) -> dict:
    seeds = jax.random.split(jax.random.key(seed), 8)
    state = scatter_about(seeds[0], (FACES, C, H, W), 1.0, 6.0, ((0, 8), (2, 8), (3, 8)))
    conv_in = scatter_about(seeds[1], (5, HID, C), (9 * C) ** -0.5, 0.1875)
    bias_in = scatter_about(seeds[2], (HID,), 0.5, 3.0, (), jnp.float32)
    conv_out = scatter_about(seeds[3], (5, C, HID), (9 * HID) ** -0.5, 0.125)
    bias_out = scatter_about(seeds[4], (C,), 0.5, 3.0, (), jnp.float32)
    land = draw_land(jax.random.fold_in(seeds[7], 71), 0)
    owner = draw_owner(jax.random.fold_in(seeds[7], 71), 0)
    return {"state": state, "conv_in": conv_in, "bias_in": bias_in, "conv_out": conv_out, "bias_out": bias_out, "land": land, "owner": owner}


OFFSETS = ((0, 0, 0), (0, 1, 1), (0, -1, 1), (1, 0, 2), (-1, 0, 2), (1, 1, 3), (-1, -1, 3), (1, -1, 4), (-1, 1, 4))


def glue_faces(values, width):
    face_count = values.shape[0]
    col_count = values.shape[3]
    east_source = values[np.arange(face_count) ^ 1]
    west_source = values[np.arange(face_count) ^ 2]
    east_strip = east_source[:, :, ::-1, col_count - width:][..., ::-1]
    west_strip = west_source[:, :, ::-1, :width][..., ::-1]
    widened = jnp.concatenate([west_strip, values, east_strip], axis=3)
    return jnp.pad(widened, ((0, 0), (0, 0), (width, width), (0, 0)))


def conv_face(padded, weights):
    row_count = padded.shape[1] - 2
    col_count = padded.shape[2] - 2
    summed = jnp.zeros((weights.shape[1], row_count, col_count), jnp.float32)
    for row_step, col_step, tap_index in OFFSETS:
        shifted = padded[:, 1 + row_step:1 + row_step + row_count, 1 + col_step:1 + col_step + col_count].astype(jnp.float32)
        summed = summed + jnp.einsum('oi,irc->orc', weights[tap_index].astype(jnp.float32), shifted)
    return summed


def reference(state, conv_in, bias_in, conv_out, bias_out, land, owner):
    padded = glue_faces(state, 1)

    def first_layer(face_block):
        return jax.nn.gelu(conv_face(face_block, conv_in) + bias_in[:, None, None]).astype(jnp.bfloat16)

    hidden = lax.map(first_layer, padded)
    hidden_padded = glue_faces(hidden, 1)

    def second_layer(pair):
        face_block, anchor = pair
        return (anchor.astype(jnp.float32) + conv_face(face_block, conv_out) + bias_out[:, None, None]).astype(jnp.bfloat16)

    new_state = lax.map(second_layer, (hidden_padded, state))
    sea = new_state[:, :OC].reshape(FACES, OC, N_ROW, RD, N_COL, WD)
    sea = sea.transpose(0, 2, 4, 1, 3, 5).reshape(FACES, TILES, OC * RD * WD)
    wet = 1 - land
    order = jnp.arange(TILES, dtype=jnp.int32)
    earlier = order[None, :] < order[:, None]
    same = (owner[:, :, None] == owner[:, None, :]) & (wet[:, None, :] == 1) & earlier[None]
    slot = jnp.sum(same.astype(jnp.int32), axis=2).astype(jnp.int32)
    target = owner * CAP + slot
    places = jnp.arange(TILES * CAP, dtype=jnp.int32)
    chosen = ((target[:, None, :] == places[None, :, None]) & (wet[:, None, :] == 1)).astype(jnp.float32)
    ocean = jnp.einsum('fst,ftk->fsk', chosen, sea.astype(jnp.float32))
    ocean = ocean.reshape(FACES, TILES, CAP, OC, RD, WD).astype(jnp.bfloat16)
    return new_state, ocean
```

```python
import jax
import jax.numpy as jnp
from jax import lax
from jax.sharding import PartitionSpec as P

OC = 4
CAP = 2
ALL = ("face", "row", "col")
CLASSES = ((3, 2, 4), (1, 0, 1), (4, 2, 3))


def exchange(values, partner):
    shape = tuple(lax.axis_size(a) for a in ALL)
    number = lambda f, r, c: (f * shape[1] + r) * shape[2] + c
    pairs = []
    for f in range(shape[0]):
        for r in range(shape[1]):
            for c in range(shape[2]):
                other = partner(f, r, c, shape)
                if other is not None:
                    pairs.append((number(f, r, c), number(*other)))
    return lax.ppermute(values, ALL, pairs)


def col_near(f, r, c, shape):
    return (f, r, c ^ 1)


def col_far(f, r, c, shape):
    if c == 0:
        return (f ^ 2, shape[1] - 1 - r, c)
    if c == shape[2] - 1:
        return (f ^ 1, shape[1] - 1 - r, c)
    return (f, r, ((c + 1) ^ 1) - 1)


def row_near(f, r, c, shape):
    return (f, r ^ 1, c)


def row_far(f, r, c, shape):
    return None if r in (0, shape[1] - 1) else (f, ((r + 1) ^ 1) - 1, c)


def extend(values, width):
    r, c = lax.axis_index("row"), lax.axis_index("col")
    east, west = values[:, :, -width:], values[:, :, :width]
    odd = c % 2 == 1
    flip = lambda v: v[:, ::-1, ::-1]
    far = jnp.where(odd, east, west)
    at_seam = (c == 0) | (c == lax.axis_size("col") - 1)
    far = jnp.where(at_seam, flip(far), far)
    got_far = exchange(far, col_far)
    got_near = exchange(jnp.where(odd, west, east), col_near)
    wide = jnp.concatenate(
        [jnp.where(odd, got_near, got_far), values, jnp.where(odd, got_far, got_near)], axis=2
    )
    top, bottom = wide[:, :width], wide[:, -width:]
    odd = r % 2 == 1
    got_far = exchange(jnp.where(odd, bottom, top), row_far)
    got_near = exchange(jnp.where(odd, top, bottom), row_near)
    return jnp.concatenate(
        [jnp.where(odd, got_near, got_far), wide, jnp.where(odd, got_far, got_near)], axis=1
    )


def conv(padded, weights):
    kernel = jnp.stack([jnp.stack([weights[t] for t in row], axis=-1) for row in CLASSES], axis=-2)
    return lax.conv_general_dilated(
        padded[None],
        kernel,
        (1, 1),
        "VALID",
        dimension_numbers=("NCHW", "OIHW", "NCHW"),
        preferred_element_type=jnp.float32,
    )[0]


def relay(sea, land, owner):
    rows, cols = lax.axis_size("row"), lax.axis_size("col")
    r, c = lax.axis_index("row"), lax.axis_index("col")
    wet = land[0] == 0
    owner = owner[0]
    order = jnp.arange(owner.shape[0], dtype=jnp.int32)
    same = (owner[:, None] == owner[None, :]) & wet[None, :] & (order[None, :] < order[:, None])
    slot = jnp.sum(same.astype(jnp.int32), axis=1)
    mine = r * cols + c
    to_col = wet[mine] & (owner[mine] % cols == jnp.arange(cols))
    sent = jnp.where(to_col[:, None, None, None], sea[None], jnp.zeros_like(sea)[None])
    held = lax.all_to_all(sent, "col", 0, 0, tiled=True)
    row_owner = lax.dynamic_slice_in_dim(owner, r * cols, cols)
    row_wet = lax.dynamic_slice_in_dim(wet, r * cols, cols)
    row_slot = lax.dynamic_slice_in_dim(slot, r * cols, cols)
    place = jnp.where(row_wet & (row_owner % cols == c), row_owner // cols * CAP + row_slot, -1)
    chosen = (place[None, :] == jnp.arange(rows * CAP)[:, None]).astype(jnp.bfloat16)
    sent = jnp.einsum("pj,jabc->pabc", chosen, held, preferred_element_type=jnp.float32)
    sent = sent.astype(jnp.bfloat16).reshape((rows, CAP) + sea.shape)
    got = lax.all_to_all(sent, "row", 0, 0, tiled=True)
    return jnp.sum(got.astype(jnp.float32), axis=0).astype(jnp.bfloat16)


def local(state, conv_in, bias_in, conv_out, bias_out, land, owner):
    anchor = state[0]
    r = lax.axis_index("row")
    hidden = jax.nn.gelu(conv(extend(anchor, 2), conv_in) + bias_in[:, None, None])
    height = hidden.shape[1]
    index = jnp.arange(height)
    inside = ((r > 0) | (index > 0)) & ((r < lax.axis_size("row") - 1) | (index < height - 1))
    hidden = jnp.where(inside[None, :, None], hidden, 0).astype(jnp.bfloat16)
    new_state = anchor.astype(jnp.float32) + conv(hidden, conv_out) + bias_out[:, None, None]
    new_state = new_state.astype(jnp.bfloat16)
    return (new_state[None], relay(new_state[:OC], land, owner)[None, None])


def solution(mesh):
    in_specs = (P("face", None, "row", "col"), P(), P(), P(), P(), P("face", None), P("face", None))
    out_specs = (P("face", None, "row", "col"), P("face", ("row", "col"), None, None, None, None))
    return jax.shard_map(local, mesh=mesh, in_specs=in_specs, out_specs=out_specs, check_vma=False)
```

```python
import jax
import jax.numpy as jnp
from jax import lax
from jax.experimental import pallas as pl
from jax.experimental.pallas import tpu as pltpu
from jax.sharding import PartitionSpec as P

OC = 4
CAP = 2
ALL = ("face", "row", "col")
BORDER = 2

PITCH = 144
TAPS = (3, 2, 4, 1, 0, 1, 4, 2, 3)
NT = (((1,), (1,)), ((), ()))
VM = pl.BlockSpec(memory_space=pltpu.VMEM)
SM = pl.BlockSpec(memory_space=pltpu.SMEM)
PARAMS = pltpu.CompilerParams(vmem_limit_bytes=28 * 2**20)


def turn_kernel(state, cells, edges, flat, turned):
    chans, rows, cols = state.shape
    flat[...] = state[...].reshape(chans * rows, cols).astype(jnp.float32)
    for r in range(rows):
        turned[r] = flat[pl.ds(r, chans, stride=rows), :].T
        cells[r] = turned[r].astype(jnp.bfloat16)
    for k, w in enumerate((0, 1, cols - 2, cols - 1)):
        edges[k] = turned.reshape(rows * cols, chans)[pl.ds(w, rows, stride=cols), :].astype(jnp.bfloat16)


def turn(state):
    chans, rows, cols = state.shape
    return pl.pallas_call(
        turn_kernel,
        out_shape=[jax.ShapeDtypeStruct((rows, cols, chans), jnp.bfloat16), jax.ShapeDtypeStruct((4, rows, chans), jnp.bfloat16)],
        in_specs=[VM], out_specs=[VM, VM],
        scratch_shapes=[pltpu.VMEM((chans * rows, cols), jnp.float32), pltpu.VMEM((rows, cols, chans), jnp.float32)],
        compiler_params=PARAMS,
    )(state)


def hidden_kernel(flags, cells, sides, above, below, conv_in, bias_in, conv_out, bias_sea, state, hidden, blocks, field, taps):
    rows, cols, chans = cells.shape
    hid = bias_in.shape[1]
    f32 = jnp.float32
    for r in range(rows):
        field[2 + r, 8 : 8 + cols] = cells[r].astype(f32)
    side = sides[...].astype(f32)
    for k, s in enumerate((6, 7, 8 + cols, 9 + cols)):
        for r in range(rows):
            field[2 + r, s : s + 1] = side[k, r : r + 1]
    for start, strip in ((0, above), (2 + rows, below)):
        v = strip[...].astype(f32)
        for j in range(2):
            field[start + j, 8 : 8 + cols] = v[j * cols : (j + 1) * cols]
            for k, s in enumerate((6, 7, 8 + cols, 9 + cols)):
                at = 2 * cols + 4 * j + k
                field[start + j, s : s + 1] = v[at : at + 1]
    for r in range(rows + 4):
        for k in range(3):
            taps[r, :, k * chans : (k + 1) * chans] = field[r, 6 + k : 6 + k + PITCH].astype(jnp.bfloat16)
    weights = jnp.concatenate([conv_in[t] for t in TAPS], axis=1)
    step = 3
    for j in range(0, rows + 2, step):
        data = jnp.concatenate([taps[j + d : j + d + step].reshape(step * PITCH, 3 * chans) for d in range(3)], axis=1)
        x = lax.dot_general(data, weights, NT, preferred_element_type=f32) + bias_in[...]
        x = jax.nn.gelu(x).reshape(step, PITCH, hid)
        for d in range(step):
            y = x[d]
            if j + d == 0:
                y = jnp.where(flags[0] == 0, 0.0, y)
            if j + d == rows + 1:
                y = jnp.where(flags[1] == 0, 0.0, y)
            hidden[j + d] = y.astype(jnp.bfloat16)
    sea_weights = conv_out[:, 0:16].reshape(5 * 16, hid)
    z = []
    for j in range(0, rows + 2, 2):
        two = lax.dot_general(sea_weights, hidden[j : j + 2].reshape(2 * PITCH, hid), NT, preferred_element_type=f32)
        z += [two[:, :PITCH], two[:, PITCH:]]
    cut = lambda j, t: z[j][16 * t : 16 * t + 8]
    count = blocks.shape[1]
    for r in range(rows):
        j = r + 1
        mid = cut(j, 0) + cut(j - 1, 2) + cut(j + 1, 2)
        plus = cut(j, 1) + cut(j + 1, 3) + cut(j - 1, 4)
        minus = cut(j, 1) + cut(j - 1, 3) + cut(j + 1, 4)
        total = mid[:, 1 : 1 + cols] + plus[:, 2 : 2 + cols] + minus[:, :cols] + bias_sea[...]
        field[0:8, r] = total
    for o in range(count):
        v = field[o, 0:rows] [:, :cols] + state[o].astype(f32)
        v = v.astype(jnp.bfloat16)
        for b in range(blocks.shape[0]):
            blocks[b, o] = jnp.where(flags[2] == b, v, jnp.zeros_like(v))


def first_half(flags, cells, sides, above, below, conv_in, bias_in, conv_out, bias_sea, state, n_blocks, n_sea):
    rows, cols, chans = cells.shape
    hid = conv_in.shape[1]
    return pl.pallas_call(
        hidden_kernel,
        out_shape=[
            jax.ShapeDtypeStruct((rows + 2, PITCH, hid), jnp.bfloat16),
            jax.ShapeDtypeStruct((n_blocks, n_sea, rows, cols), jnp.bfloat16),
        ],
        in_specs=[SM] + [VM] * 9,
        out_specs=[VM, VM],
        scratch_shapes=[
            pltpu.VMEM((rows + 4, PITCH + 8, chans), jnp.float32),
            pltpu.VMEM((rows + 4, PITCH, 3 * chans), jnp.bfloat16),
        ],
        compiler_params=PARAMS,
        cost_estimate=pl.CostEstimate(flops=2 * 2592 * 1152 * 256, bytes_accessed=3_000_000, transcendentals=2592 * 256),
    )(flags, cells, sides, above, below, conv_in, bias_in, conv_out, bias_sea, state)


def out_kernel(hidden, cells, conv_out, bias_out, new_state, z, flat):
    rows, cols, chans = cells.shape
    hid = hidden.shape[2]
    f32 = jnp.float32
    weights = conv_out[...].reshape(5 * chans, hid)
    step = 3
    for j in range(0, rows + 2, step):
        data = hidden[j : j + step].reshape(step * PITCH, hid)
        z[j : j + step] = lax.dot_general(data, weights, NT, preferred_element_type=f32).reshape(step, PITCH, 5 * chans)
    cut = lambda j, t, s: z[j, s : s + cols, t * chans : (t + 1) * chans]
    for r in range(rows):
        j = r + 1
        total = cut(j, 0, 1) + cut(j - 1, 2, 1) + cut(j + 1, 2, 1)
        total += cut(j, 1, 2) + cut(j + 1, 3, 2) + cut(j - 1, 4, 2)
        total += cut(j, 1, 0) + cut(j - 1, 3, 0) + cut(j + 1, 4, 0)
        total += bias_out[...] + cells[r].astype(f32)
        flat[pl.ds(r, chans, stride=rows), :] = total.T
    new_state[...] = flat[...].reshape(chans, rows, cols).astype(jnp.bfloat16)


def second_half(hidden, cells, conv_out, bias_out):
    rows, cols, chans = cells.shape
    return pl.pallas_call(
        out_kernel,
        out_shape=jax.ShapeDtypeStruct((chans, rows, cols), jnp.bfloat16),
        in_specs=[VM] * 4,
        out_specs=VM,
        scratch_shapes=[pltpu.VMEM((rows + 2, PITCH, 5 * chans), jnp.float32), pltpu.VMEM((chans * rows, cols), jnp.float32)],
        compiler_params=PARAMS,
        cost_estimate=pl.CostEstimate(flops=2 * 2592 * 640 * 256, bytes_accessed=2_500_000, transcendentals=0),
    )(hidden, cells, conv_out, bias_out)


def exchange(values, partner):
    shape = tuple(lax.axis_size(a) for a in ALL)
    number = lambda f, r, c: (f * shape[1] + r) * shape[2] + c
    pairs = []
    for f in range(shape[0]):
        for r in range(shape[1]):
            for c in range(shape[2]):
                other = partner(f, r, c, shape)
                if other is not None:
                    pairs.append((number(f, r, c), number(*other)))
    return lax.ppermute(values, ALL, pairs)


def col_near(f, r, c, shape):
    return (f, r, c ^ 1)


def col_far(f, r, c, shape):
    if c == 0:
        return (f ^ 2, shape[1] - 1 - r, c)
    if c == shape[2] - 1:
        return (f ^ 1, shape[1] - 1 - r, c)
    return (f, r, ((c + 1) ^ 1) - 1)


def row_near(f, r, c, shape):
    return (f, r ^ 1, c)


def row_far(f, r, c, shape):
    return None if r in (0, shape[1] - 1) else (f, ((r + 1) ^ 1) - 1, c)


def sort_kernel(place, held, sent):
    sent[...] = jnp.zeros_like(sent)
    for k in range(held.shape[0]):

        @pl.when(place[k] >= 0)
        def _():
            sent[pl.ds(place[k], 1)] = held[k][None]


def sort_tiles(place, held, count):
    return pl.pallas_call(
        sort_kernel,
        out_shape=jax.ShapeDtypeStruct((count,) + held.shape[1:], held.dtype),
        in_specs=[SM, VM],
        out_specs=VM,
        compiler_params=PARAMS,
    )(place, held)


def merge_kernel(got, ocean):
    total = got[0].astype(jnp.float32)
    for k in range(1, got.shape[0]):
        total += got[k].astype(jnp.float32)
    ocean[...] = total.astype(ocean.dtype)


def merge(got):
    return pl.pallas_call(
        merge_kernel,
        out_shape=jax.ShapeDtypeStruct(got.shape[1:], got.dtype),
        in_specs=[VM],
        out_specs=VM,
        compiler_params=PARAMS,
    )(got)


def routes(land, owner):
    rows, cols = lax.axis_size("row"), lax.axis_size("col")
    r, c = lax.axis_index("row"), lax.axis_index("col")
    wet = land[0] == 0
    owner = owner[0]
    order = jnp.arange(owner.shape[0], dtype=jnp.int32)
    same = (owner[:, None] == owner[None, :]) & wet[None, :] & (order[None, :] < order[:, None])
    slot = jnp.sum(same.astype(jnp.int32), axis=1)
    mine = (order == r * cols + c) & wet
    to_col = jnp.sum(jnp.where(mine, owner % cols + 1, 0)) - 1
    place = jnp.where(wet & (owner % cols == c), owner // cols * CAP + slot, -1)
    place = lax.dynamic_slice_in_dim(place, r * cols, cols)
    return to_col, jnp.where(place < rows * CAP, place, -1)


def local(state, conv_in, bias_in, conv_out, bias_out, land, owner):
    state = state[0]
    chans, height, width = state.shape
    rows, cols = lax.axis_size("row"), lax.axis_size("col")
    r, c = lax.axis_index("row"), lax.axis_index("col")
    cells, edges = turn(state)

    odd = c % 2 == 1
    west, east = edges[:BORDER], edges[BORDER:]
    flip = lambda v: v[::-1, ::-1]
    far = jnp.where(odd, east, west)
    far = jnp.where((c == 0) | (c == cols - 1), flip(far), far)
    got_far = exchange(far, col_far)
    got_near = exchange(jnp.where(odd, west, east), col_near)
    sides = jnp.concatenate([jnp.where(odd, got_near, got_far), jnp.where(odd, got_far, got_near)])

    odd = r % 2 == 1

    def strip(start):
        corners = sides[:, start : start + BORDER].transpose(1, 0, 2)
        body = cells[start : start + BORDER].reshape(BORDER * width, chans)
        return jnp.concatenate([body, corners.reshape(2 * BORDER * BORDER, chans)])

    top, bottom = strip(0), strip(height - BORDER)
    got_far = exchange(jnp.where(odd, bottom, top), row_far)
    got_near = exchange(jnp.where(odd, top, bottom), row_near)
    above, below = jnp.where(odd, got_near, got_far), jnp.where(odd, got_far, got_near)

    to_col, place = routes(land, owner)
    flags = jnp.stack([r > 0, r < rows - 1, to_col]).astype(jnp.int32)
    hidden, blocks = first_half(
        flags, cells, sides, above, below, conv_in, bias_in[None], conv_out, bias_out[:8, None], state, cols, OC
    )
    held = lax.all_to_all(blocks, "col", 0, 0, tiled=True)
    new_state = second_half(hidden, cells, conv_out, bias_out[None])
    sent = sort_tiles(place, held, rows * CAP).reshape((rows, CAP, OC, height, width))
    got = lax.all_to_all(sent, "row", 0, 0, tiled=True)
    return (new_state[None], merge(got)[None, None])


def solution(mesh):
    in_specs = (P("face", None, "row", "col"), P(), P(), P(), P(), P("face", None), P("face", None))
    out_specs = (P("face", None, "row", "col"), P("face", ("row", "col"), None, None, None, None))
    return jax.shard_map(local, mesh=mesh, in_specs=in_specs, out_specs=out_specs, check_vma=False)
```

```python
import jax
import jax.numpy as jnp
from jax import lax
from jax.experimental import pallas as pl
from jax.experimental.pallas import tpu as pltpu
from jax.sharding import PartitionSpec as P

OC = 4
CAP = 2
ALL = ("face", "row", "col")
BORDER = 2
LONG = 32
TAPS = (3, 2, 4, 1, 0, 1, 4, 2, 3)
NT = (((1,), (1,)), ((), ()))
VM = pl.BlockSpec(memory_space=pltpu.VMEM)
PARAMS = pltpu.CompilerParams(vmem_limit_bytes=24 * 2**20)
F32 = jnp.float32
BF16 = jnp.bfloat16


def call(kernel, out_shape, scratch, cost, *operands):
    many = isinstance(out_shape, list)
    return pl.pallas_call(
        kernel,
        out_shape=out_shape,
        in_specs=[VM] * len(operands),
        out_specs=[VM] * len(out_shape) if many else VM,
        scratch_shapes=[pltpu.VMEM(s, d) for s, d in scratch],
        compiler_params=PARAMS,
        cost_estimate=pl.CostEstimate(flops=cost[0], bytes_accessed=cost[1], transcendentals=cost[2]),
    )(*operands)


def turn_kernel(state, cells, edges, flat, turned):
    chans, rows, cols = state.shape
    flat[...] = state[...].reshape(chans * rows, cols).astype(F32)
    for r in range(rows):
        turned[r] = flat[pl.ds(r, chans, stride=rows), :].T
        cells[r] = turned[r].astype(BF16)
    for k, w in enumerate((0, 1, cols - 2, cols - 1)):
        edges[k] = turned.reshape(rows * cols, chans)[pl.ds(w, rows, stride=cols), :].astype(BF16)


def turn(state):
    chans, rows, cols = state.shape
    return call(
        turn_kernel,
        [jax.ShapeDtypeStruct((rows, cols, chans), BF16), jax.ShapeDtypeStruct((4, rows, chans), BF16)],
        [((chans * rows, cols), F32), ((rows, cols, chans), F32)],
        (0, 4 * state.size, 0),
        state,
    )


def route_kernel(owner, land, here, target, place):
    count = owner.shape[1]
    cols = rows = 8
    wide = lambda v: jnp.broadcast_to(v, (count, count))
    i = lax.broadcasted_iota(jnp.int32, (count, count), 0)
    j = lax.broadcasted_iota(jnp.int32, (count, count), 1)
    own, wet = wide(owner[...]), wide(1 - land[...])
    down = lambda v: jnp.sum(jnp.where(i == j, v, 0).astype(F32), axis=1, keepdims=True)
    own_i, wet_i = down(own), down(wet)
    same = (own.astype(F32) == own_i) & (wet == 1) & (j < i)
    slot = jnp.sum(jnp.where(same, 1.0, 0.0), axis=1, keepdims=True)
    lanes = here.shape[1]
    spread = lambda v: jnp.broadcast_to(v, (count, lanes))
    own_i, wet_i, slot = spread(own_i).astype(jnp.int32), spread(wet_i), spread(slot).astype(jnp.int32)
    tile = lax.broadcasted_iota(jnp.int32, (count, lanes), 0)
    r, c = here[2:3], here[3:4]
    mine = (tile == r * cols + c) & (wet_i > 0)
    to_col = jnp.sum(jnp.where(mine, (own_i & (cols - 1)) + 1, 0).astype(F32), axis=0, keepdims=True) - 1.0
    target[...] = jnp.broadcast_to(to_col, target.shape)
    spot = jnp.where((wet_i > 0) & ((own_i & (cols - 1)) == c), (own_i >> 3) * 2 + slot, -1).astype(F32)
    total = jnp.full((cols, lanes), 0.0, F32)
    for k in range(rows):
        total = jnp.where(r == k, spot[k * cols : (k + 1) * cols], total)
    place[...] = total


def routes(owner, land, here):
    shape = jax.ShapeDtypeStruct((8, here.shape[1]), F32)
    return call(route_kernel, [shape, shape], [], (100000, 20000, 0), owner, land, here)


def inner_kernel(here, cells, above, below, conv_in, bias_in, conv_out, bias_sea, state, hidden, sea, field, taps):
    rows, cols, chans = cells.shape
    hid = bias_in.shape[1]
    for start, part in ((0, above), (BORDER, cells), (BORDER + rows, below)):
        for r in range(part.shape[0]):
            field[start + r, 8 : 8 + cols] = part[r].astype(F32)
    for r in range(rows + 2 * BORDER):
        for k in range(3):
            taps[r, :, k * chans : (k + 1) * chans] = field[r, 7 + k : 7 + k + cols].astype(BF16)
    weights = jnp.concatenate([conv_in[t] for t in TAPS], axis=1)
    col = lax.broadcasted_iota(jnp.int32, (cols, hid), 0)
    inside = (col > 0) & (col < cols - 1)
    keep = jnp.concatenate([here[0:2]] * (hid // here.shape[1]), axis=1) > 0
    step = 3
    for j in range(0, rows + 2, step):
        data = jnp.concatenate([taps[j + d : j + d + step].reshape(step * cols, 3 * chans) for d in range(3)], axis=1)
        x = lax.dot_general(data, weights, NT, preferred_element_type=F32) + bias_in[...]
        x = jax.nn.gelu(x).reshape(step, cols, hid)
        for d in range(step):
            here_in = inside
            if j + d == 0:
                here_in = inside & keep[0:1]
            if j + d == rows + 1:
                here_in = inside & keep[1:2]
            hidden[j + d] = jnp.where(here_in, x[d], 0.0).astype(BF16)
    sea_weights = conv_out[:, 0:16].reshape(5 * 16, hid)
    z = []
    for j in range(0, rows + 2, 2):
        two = lax.dot_general(sea_weights, hidden[j : j + 2].reshape(2 * cols, hid), NT, preferred_element_type=F32)
        z += [two[:, :cols], two[:, cols:]]
    cut = lambda j, t: z[j][16 * t : 16 * t + 8]
    for r in range(rows):
        j = r + 1
        mid = cut(j, 0) + cut(j - 1, 2) + cut(j + 1, 2)
        plus = cut(j, 1) + cut(j + 1, 3) + cut(j - 1, 4)
        minus = cut(j, 1) + cut(j - 1, 3) + cut(j + 1, 4)
        total = mid + pltpu.roll(plus, cols - 1, 1) + pltpu.roll(minus, 1, 1) + bias_sea[...]
        sea[:, r] = total
    sea[...] += state[0:8].astype(F32)


def inner_part(here, cells, above, below, conv_in, bias_in, conv_out, bias_sea, state):
    rows, cols, chans = cells.shape
    hid = conv_in.shape[1]
    return call(
        inner_kernel,
        [jax.ShapeDtypeStruct((rows + 2, cols, hid), BF16), jax.ShapeDtypeStruct((8, rows, cols), F32)],
        [((rows + 4, cols + 16, chans), F32), ((rows + 4, cols, 3 * chans), BF16)],
        (2 * 18 * 128 * (1152 + 80) * 256, 3000000, 18 * 128 * 256),
        here, cells, above, below, conv_in, bias_in, conv_out, bias_sea, state,
    )


def rim_kernel(here, target, edges, sides, conv_in, bias_in, conv_out, sea, rim, blocks, field, tall):
    hid = bias_in.shape[1]
    n_blocks, n_sea, rows, cols = blocks.shape
    for k, (part, at) in enumerate(((sides, 0), (sides, 1), (edges, 0), (edges, 1), (edges, 2), (edges, 3), (sides, 2), (sides, 3))):
        field[k, 0:LONG] = part[at].astype(F32)
        field[k, LONG : LONG + 8] = jnp.zeros((8, field.shape[2]), F32)
    weights = jnp.concatenate([conv_in[t] for t in TAPS], axis=1)
    data = []
    for k in (1, 2, 5, 6):
        data.append(jnp.concatenate([field[k + dc, dr : dr + LONG].astype(BF16) for dr in range(3) for dc in (-1, 0, 1)], axis=1))
    x = lax.dot_general(jnp.concatenate(data, axis=0), weights, NT, preferred_element_type=F32) + bias_in[...]
    x = jax.nn.gelu(x)
    keep = jnp.concatenate([here[0:2]] * (hid // here.shape[1]), axis=1) > 0
    row = lax.broadcasted_iota(jnp.int32, (LONG, hid), 0)
    inside = ((row > 0) | keep[0:1]) & ((row < rows + 1) | keep[1:2]) & (row < rows + 2)
    for k in range(4):
        tall[k] = jnp.where(inside, x[k * LONG : (k + 1) * LONG], 0.0).astype(BF16).astype(F32)
        rim[k] = tall[k].astype(BF16)
    data = [jnp.concatenate([tall[k, d : d + rows].astype(BF16) for d in range(3)], axis=1) for k in range(4)]
    part = lambda dc: jnp.concatenate([conv_out[TAPS[3 * dr + dc], 0:16] for dr in range(3)], axis=1)
    sea_weights = jnp.concatenate([part(dc) for dc in range(3)], axis=0)
    z = lax.dot_general(jnp.concatenate(data, axis=0), sea_weights, NT, preferred_element_type=F32)
    lane = lax.broadcasted_iota(jnp.int32, (rows, cols), 1)
    for o in range(n_sea):
        piece = lambda k, dc: z[k * rows : (k + 1) * rows, 16 * (dc + 1) + o : 16 * (dc + 1) + o + 1]
        extra = jnp.where(lane == 0, piece(0, -1) + piece(1, 0), 0.0)
        extra = jnp.where(lane == 1, piece(1, -1), extra)
        extra = jnp.where(lane == cols - 2, piece(2, 1), extra)
        extra = jnp.where(lane == cols - 1, piece(2, 0) + piece(3, 1), extra)
        v = (sea[o] + extra).astype(BF16).astype(F32)
        for b in range(n_blocks):
            blocks[b, o] = jnp.where(target[0:1] == b, v, 0.0).astype(BF16)


def rim_part(here, target, edges, sides, conv_in, bias_in, conv_out, sea, n_blocks, n_sea):
    rows, cols = sea.shape[1:]
    chans = edges.shape[2]
    hid = conv_in.shape[1]
    return call(
        rim_kernel,
        [jax.ShapeDtypeStruct((4, LONG, hid), BF16), jax.ShapeDtypeStruct((n_blocks, n_sea, rows, cols), BF16)],
        [((8, LONG + 8, chans), F32), ((4, LONG, hid), F32)],
        (2 * 128 * 1152 * 256, 1500000, 128 * 256),
        here, target, edges, sides, conv_in, bias_in, conv_out, sea,
    )


def out_kernel(hidden, rim, cells, conv_out, bias_out, new_state, z, flat):
    rows, cols, chans = cells.shape
    hid = hidden.shape[2]
    weights = conv_out[...].reshape(5 * chans, hid)
    step = 3
    for j in range(0, rows + 2, step):
        data = hidden[j : j + step].reshape(step * cols, hid)
        got = lax.dot_general(data, weights, NT, preferred_element_type=F32)
        z[j : j + step, 8 : 8 + cols] = got.reshape(step, cols, 5 * chans)
    got = lax.dot_general(rim[...].reshape(4 * LONG, hid), weights, NT, preferred_element_type=F32)
    for k, s in enumerate((7, 8, 7 + cols, 8 + cols)):
        for j in range(rows + 2):
            z[j, s : s + 1] = got[k * LONG + j : k * LONG + j + 1]
    cut = lambda j, t, s: z[j, 8 + s : 8 + s + cols, t * chans : (t + 1) * chans]
    for r in range(rows):
        j = r + 1
        total = cut(j, 0, 0) + cut(j - 1, 2, 0) + cut(j + 1, 2, 0)
        total += cut(j, 1, 1) + cut(j + 1, 3, 1) + cut(j - 1, 4, 1)
        total += cut(j, 1, -1) + cut(j - 1, 3, -1) + cut(j + 1, 4, -1)
        total += bias_out[...] + cells[r].astype(F32)
        flat[pl.ds(r, chans, stride=rows), :] = total.T
    new_state[...] = flat[...].reshape(chans, rows, cols).astype(BF16)


def out_part(hidden, rim, cells, conv_out, bias_out):
    rows, cols, chans = cells.shape
    return call(
        out_kernel,
        jax.ShapeDtypeStruct((chans, rows, cols), BF16),
        [((rows + 2, cols + 16, 5 * chans), F32), ((chans * rows, cols), F32)],
        (2 * 18 * 128 * 640 * 256, 3000000, 0),
        hidden, rim, cells, conv_out, bias_out,
    )


def sort_kernel(place, held, sent):
    half = sent.shape[0] // 2
    parts = [held[k].astype(F32) for k in range(held.shape[0])]
    for p in range(half):
        total = jnp.zeros_like(parts[0])
        for k, v in enumerate(parts):
            total = jnp.where((place[k : k + 1] == p)[None], v, total)
        sent[p] = total.astype(BF16)
    sent[half:] = jnp.zeros((half,) + sent.shape[1:], BF16)


def sort_tiles(place, held, count):
    shape = jax.ShapeDtypeStruct((count,) + held.shape[1:], BF16)
    return call(sort_kernel, shape, [], (100000, 6 * held.size, 0), place, held)


def merge_kernel(got, ocean):
    total = got[0].astype(F32)
    for k in range(1, got.shape[0]):
        total += got[k].astype(F32)
    ocean[...] = total.astype(BF16)


def merge(got):
    return call(merge_kernel, jax.ShapeDtypeStruct(got.shape[1:], BF16), [], (100000, 2 * got.size, 0), got)


def exchange(values, partner):
    shape = tuple(lax.axis_size(a) for a in ALL)
    number = lambda f, r, c: (f * shape[1] + r) * shape[2] + c
    pairs = []
    for f in range(shape[0]):
        for r in range(shape[1]):
            for c in range(shape[2]):
                other = partner(f, r, c, shape)
                if other is not None:
                    pairs.append((number(f, r, c), number(*other)))
    return lax.ppermute(values, ALL, pairs)


def col_near(f, r, c, shape):
    return (f, r, c ^ 1)


def col_far(f, r, c, shape):
    if c == 0:
        return (f ^ 2, shape[1] - 1 - r, c)
    if c == shape[2] - 1:
        return (f ^ 1, shape[1] - 1 - r, c)
    return (f, r, ((c + 1) ^ 1) - 1)


def row_near(f, r, c, shape):
    return (f, r ^ 1, c)


def row_far(f, r, c, shape):
    return None if r in (0, shape[1] - 1) else (f, ((r + 1) ^ 1) - 1, c)


def local(state, conv_in, bias_in, conv_out, bias_out, land, owner):
    state = state[0]
    chans, height, width = state.shape
    rows, cols = lax.axis_size("row"), lax.axis_size("col")
    r, c = lax.axis_index("row"), lax.axis_index("col")
    lines = (r > 0, r < rows - 1, r, c, 0, 0, 0, 0)
    here = jnp.concatenate([jnp.full((1, 128), v, jnp.int32) for v in lines])
    cells, edges = turn(state)

    odd = r % 2 == 1
    top, bottom = cells[:BORDER], cells[height - BORDER :]
    got_far = exchange(jnp.where(odd, bottom, top), row_far)
    got_near = exchange(jnp.where(odd, top, bottom), row_near)
    above, below = jnp.where(odd, got_near, got_far), jnp.where(odd, got_far, got_near)

    odd = c % 2 == 1
    pick = lambda v: jnp.stack([v[:, 0], v[:, 1], v[:, width - 2], v[:, width - 1]])
    tall = jnp.concatenate([pick(above), edges, pick(below)], axis=1)
    full = lambda v: jnp.pad(v, ((0, 0), (0, LONG - v.shape[1]), (0, 0)))
    west, east = tall[:BORDER], tall[BORDER:]
    far = jnp.where(odd, east, west)
    far = jnp.where((c == 0) | (c == cols - 1), far[::-1, ::-1], far)
    got_far = exchange(full(far), col_far)
    got_near = exchange(full(jnp.where(odd, west, east)), col_near)
    sides = jnp.concatenate([jnp.where(odd, got_near, got_far), jnp.where(odd, got_far, got_near)])

    target, place = routes(owner, land, here)
    bias_in = bias_in[None]
    hidden, sea = inner_part(here, cells, above, below, conv_in, bias_in, conv_out, bias_out[:8, None], state)
    rim, blocks = rim_part(here, target, full(tall), sides, conv_in, bias_in, conv_out, sea, cols, OC)
    held = lax.all_to_all(blocks, "col", 0, 0, tiled=True)
    new_state = out_part(hidden, rim, cells, conv_out, bias_out[None])
    sent = sort_tiles(place, held, rows * CAP).reshape((rows, CAP, OC, height, width))
    got = lax.all_to_all(sent, "row", 0, 0, tiled=True)
    return (new_state[None], merge(got)[None, None])


def solution(mesh):
    in_specs = (P("face", None, "row", "col"), P(), P(), P(), P(), P("face", None), P("face", None))
    out_specs = (P("face", None, "row", "col"), P("face", ("row", "col"), None, None, None, None))
    return jax.shard_map(local, mesh=mesh, in_specs=in_specs, out_specs=out_specs, check_vma=False)
```

```python
import jax
import jax.numpy as jnp
from jax import lax
from jax.experimental import pallas as pl
from jax.experimental.pallas import tpu as pltpu
from jax.sharding import PartitionSpec as P

OC = 4
CAP = 2
ALL = ("face", "row", "col")
BORDER = 2
LONG = 32
TAPS = (3, 2, 4, 1, 0, 1, 4, 2, 3)
NT = (((1,), (1,)), ((), ()))
VM = pl.BlockSpec(memory_space=pltpu.VMEM)
F32 = jnp.float32
BF16 = jnp.bfloat16


def call(kernel, out_shape, scratch, cost, room, *operands):
    many = isinstance(out_shape, list)
    return pl.pallas_call(
        kernel,
        out_shape=out_shape,
        in_specs=[VM] * len(operands),
        out_specs=[VM] * len(out_shape) if many else VM,
        scratch_shapes=[pltpu.VMEM(s, d) for s, d in scratch],
        compiler_params=pltpu.CompilerParams(vmem_limit_bytes=room * 2**20),
        cost_estimate=pl.CostEstimate(flops=cost[0], bytes_accessed=cost[1], transcendentals=cost[2]),
    )(*operands)


def turn_kernel(here, state, cells, edges, far, near, first, flat, turned):
    chans, rows, cols = state.shape
    flat[...] = state[...].reshape(chans * rows, cols).astype(F32)
    for r in range(rows):
        turned[r] = flat[pl.ds(r, chans, stride=rows), :].T
        cells[r] = turned[r].astype(BF16)
    for k, w in enumerate((0, 1, cols - 2, cols - 1)):
        edges[k] = turned.reshape(rows * cols, chans)[pl.ds(w, rows, stride=cols), :].astype(BF16)
    odd = jnp.broadcast_to((here[2:3] & 1) == 1, (cols, chans))
    ends = (0, 1, cols - 2, cols - 1)
    lines = lambda r: [turned[r + k, w : w + 1] for w in ends for k in range(BORDER)]
    rest = jnp.zeros((8, chans), F32)
    top, bottom = (jnp.concatenate(lines(r) + [rest]) for r in (0, rows - BORDER))
    far[BORDER * cols :] = jnp.where(odd[:16], bottom, top).astype(BF16)
    near[BORDER * cols :] = jnp.where(odd[:16], top, bottom).astype(BF16)
    for k in range(BORDER):
        top, bottom = turned[k], turned[rows - BORDER + k]
        far[k * cols : (k + 1) * cols] = jnp.where(odd, bottom, top).astype(BF16)
        near[k * cols : (k + 1) * cols] = jnp.where(odd, top, bottom).astype(BF16)
    first[...] = state[0:8].astype(F32)


def turn(here, state):
    chans, rows, cols = state.shape
    strip = jax.ShapeDtypeStruct((BORDER * cols + 16, chans), BF16)
    return call(
        turn_kernel,
        [jax.ShapeDtypeStruct((rows, cols, chans), BF16), jax.ShapeDtypeStruct((4, rows, chans), BF16), strip, strip]
        + [jax.ShapeDtypeStruct((8, rows, cols), F32)],
        [((chans * rows, cols), F32), ((rows, cols, chans), F32)],
        (0, 4 * state.size, 0),
        10,
        here,
        state,
    )


def route_kernel(table, here, target, place):
    count = table.shape[1]
    cols = rows = 8
    wide = lambda v: jnp.broadcast_to(v, (count, count))
    i = lax.broadcasted_iota(jnp.int32, (count, count), 0)
    j = lax.broadcasted_iota(jnp.int32, (count, count), 1)
    own, wet = wide(table[0:1]), wide(1 - table[1:2])
    down = lambda v: jnp.sum(jnp.where(i == j, v, 0).astype(F32), axis=1, keepdims=True)
    own_i, wet_i = down(own), down(wet)
    same = (own.astype(F32) == own_i) & (wet == 1) & (j < i)
    slot = jnp.sum(jnp.where(same, 1.0, 0.0), axis=1, keepdims=True)
    lanes = here.shape[1]
    spread = lambda v: jnp.broadcast_to(v, (count, lanes))
    own_i, wet_i, slot = spread(own_i).astype(jnp.int32), spread(wet_i), spread(slot).astype(jnp.int32)
    tile = lax.broadcasted_iota(jnp.int32, (count, lanes), 0)
    r, c = here[2:3], here[3:4]
    mine = (tile == r * cols + c) & (wet_i > 0)
    to_col = jnp.sum(jnp.where(mine, (own_i & (cols - 1)) + 1, 0).astype(F32), axis=0, keepdims=True) - 1.0
    target[...] = jnp.broadcast_to(to_col, target.shape)
    spot = jnp.where((wet_i > 0) & ((own_i & (cols - 1)) == c), (own_i >> 3) * 2 + slot, -1).astype(F32)
    total = jnp.full((cols, lanes), 0.0, F32)
    for k in range(rows):
        total = jnp.where(r == k, spot[k * cols : (k + 1) * cols], total)
    for k in range(cols):
        place[k] = jnp.broadcast_to(total[k : k + 1], place.shape[1:])


def routes(table, here):
    lanes = here.shape[1]
    shapes = [jax.ShapeDtypeStruct((8, lanes), F32), jax.ShapeDtypeStruct((8, 8, lanes), F32)]
    return call(route_kernel, shapes, [], (100000, 50000, 0), 4, table, here)


def strip_kernel(here, edges, got_far, got_near, tall, far, near, field, picked):
    count, rows, chans = edges.shape
    length = rows + 2 * BORDER
    odd_row = jnp.broadcast_to((here[2:3] & 1) == 1, (16, chans))
    tail = got_far.shape[0] - 16
    a, b = got_far[tail:].astype(F32), got_near[tail:].astype(F32)
    above, below = jnp.where(odd_row, b, a), jnp.where(odd_row, a, b)
    for k in range(count):
        field[k, 0:BORDER] = above[BORDER * k : BORDER * (k + 1)]
        field[k, BORDER : BORDER + rows] = edges[k].astype(F32)
        field[k, BORDER + rows : length] = below[BORDER * k : BORDER * (k + 1)]
        field[k, length:] = jnp.zeros((field.shape[1] - length, chans), F32)
        tall[k] = field[k].astype(BF16)
    col = jnp.broadcast_to(here[3:4], (LONG, chans))
    odd = (col & 1) == 1
    seam = (col == 0) | (col == here[4:5])
    for k in range(BORDER):
        west, east = field[k], field[BORDER + k]
        near[k] = jnp.where(odd, west, east).astype(BF16)
        picked[k] = jnp.where(odd, east, west)
    for k in range(BORDER):
        for r in range(length):
            field[k, r : r + 1] = picked[BORDER - 1 - k, length - 1 - r : length - r]
    for k in range(BORDER):
        far[k] = jnp.where(seam, field[k], picked[k]).astype(BF16)


def strips(here, edges, got_far, got_near):
    count, rows, chans = edges.shape
    two = jax.ShapeDtypeStruct((BORDER, LONG, chans), BF16)
    return call(
        strip_kernel,
        [jax.ShapeDtypeStruct((count, LONG, chans), BF16), two, two],
        [((count, LONG, chans), F32), ((BORDER, LONG, chans), F32)],
        (0, 200000, 0),
        4,
        here, edges, got_far, got_near,
    )


def inner_kernel(here, cells, got_far, got_near, conv_in, bias_in, conv_out, bias_out, first, hidden, sea, field, taps):
    rows, cols, chans = cells.shape
    hid = bias_in.shape[1]
    for r in range(rows):
        field[BORDER + r, 8 : 8 + cols] = cells[r].astype(F32)
    odd = jnp.broadcast_to((here[2:3] & 1) == 1, (cols, chans))
    for k in range(BORDER):
        far, near = (v[k * cols : (k + 1) * cols].astype(F32) for v in (got_far, got_near))
        field[k, 8 : 8 + cols] = jnp.where(odd, near, far)
        field[BORDER + rows + k, 8 : 8 + cols] = jnp.where(odd, far, near)
    for r in range(rows + 2 * BORDER):
        for k in range(3):
            taps[r, :, k * chans : (k + 1) * chans] = field[r, 7 + k : 7 + k + cols].astype(BF16)
    weights = jnp.concatenate([conv_in[t] for t in TAPS], axis=1)
    col = lax.broadcasted_iota(jnp.int32, (cols, hid), 0)
    inside = (col > 0) & (col < cols - 1)
    keep = jnp.concatenate([here[0:2]] * (hid // here.shape[1]), axis=1) > 0
    step = 3
    for j in range(0, rows + 2, step):
        data = jnp.concatenate([taps[j + d : j + d + step].reshape(step * cols, 3 * chans) for d in range(3)], axis=1)
        x = lax.dot_general(data, weights, NT, preferred_element_type=F32) + bias_in[...]
        x = jax.nn.gelu(x).reshape(step, cols, hid)
        for d in range(step):
            here_in = inside
            if j + d == 0:
                here_in = inside & keep[0:1]
            if j + d == rows + 1:
                here_in = inside & keep[1:2]
            hidden[j + d] = jnp.where(here_in, x[d], 0.0).astype(BF16)
    sea_weights = conv_out[:, 0:16].reshape(5 * 16, hid)
    z = []
    for j in range(0, rows + 2, 2):
        two = lax.dot_general(sea_weights, hidden[j : j + 2].reshape(2 * cols, hid), NT, preferred_element_type=F32)
        z += [two[:, :cols], two[:, cols:]]
    cut = lambda j, t: z[j][16 * t : 16 * t + 8]
    upper = bias_out[:, :128]
    lane = lax.broadcasted_iota(jnp.int32, (8, upper.shape[1]), 1)
    channel = lax.broadcasted_iota(jnp.int32, (8, upper.shape[1]), 0)
    bias_sea = jnp.sum(jnp.where(lane == channel, upper, 0.0), axis=1, keepdims=True)
    for r in range(rows):
        j = r + 1
        mid = cut(j, 0) + cut(j - 1, 2) + cut(j + 1, 2)
        plus = cut(j, 1) + cut(j + 1, 3) + cut(j - 1, 4)
        minus = cut(j, 1) + cut(j - 1, 3) + cut(j + 1, 4)
        total = mid + pltpu.roll(plus, cols - 1, 1) + pltpu.roll(minus, 1, 1) + bias_sea
        sea[:, r] = total
    sea[...] += first[...]


def inner_part(here, cells, got_far, got_near, conv_in, bias_in, conv_out, bias_out, first):
    rows, cols, chans = cells.shape
    hid = conv_in.shape[1]
    return call(
        inner_kernel,
        [jax.ShapeDtypeStruct((rows + 2, cols, hid), BF16), jax.ShapeDtypeStruct((8, rows, cols), F32)],
        [((rows + 4, cols + 16, chans), F32), ((rows + 4, cols, 3 * chans), BF16)],
        (2 * 18 * 128 * (1152 + 80) * 256, 3000000, 18 * 128 * 256),
        14,
        here, cells, got_far, got_near, conv_in, bias_in, conv_out, bias_out, first,
    )


def rim_kernel(here, target, edges, far, near, conv_in, bias_in, conv_out, sea, rim, blocks, field, tall):
    hid = bias_in.shape[1]
    n_blocks, n_sea, rows, cols = blocks.shape
    odd = jnp.broadcast_to((here[3:4] & 1) == 1, (LONG, field.shape[2]))
    for k, w in enumerate((-1, -1, 0, 1, 2, 3, -1, -1)):
        if w >= 0:
            field[k, 0:LONG] = edges[w].astype(F32)
        else:
            i, j = (k, k) if k < 2 else (k - 6, k - 4)
            one, two = far[i].astype(F32), near[j].astype(F32)
            field[k, 0:LONG] = jnp.where(odd, two, one) if k < 2 else jnp.where(odd, one, two)
        field[k, LONG : LONG + 8] = jnp.zeros((8, field.shape[2]), F32)
    weights = jnp.concatenate([conv_in[t] for t in TAPS], axis=1)
    data = []
    for k in (1, 2, 5, 6):
        data.append(jnp.concatenate([field[k + dc, dr : dr + LONG].astype(BF16) for dr in range(3) for dc in (-1, 0, 1)], axis=1))
    x = lax.dot_general(jnp.concatenate(data, axis=0), weights, NT, preferred_element_type=F32) + bias_in[...]
    x = jax.nn.gelu(x)
    keep = jnp.concatenate([here[0:2]] * (hid // here.shape[1]), axis=1) > 0
    row = lax.broadcasted_iota(jnp.int32, (LONG, hid), 0)
    inside = ((row > 0) | keep[0:1]) & ((row < rows + 1) | keep[1:2]) & (row < rows + 2)
    for k in range(4):
        tall[k] = jnp.where(inside, x[k * LONG : (k + 1) * LONG], 0.0).astype(BF16).astype(F32)
        rim[k] = tall[k].astype(BF16)
    data = [jnp.concatenate([tall[k, d : d + rows].astype(BF16) for d in range(3)], axis=1) for k in range(4)]
    part = lambda dc: jnp.concatenate([conv_out[TAPS[3 * dr + dc], 0:16] for dr in range(3)], axis=1)
    sea_weights = jnp.concatenate([part(dc) for dc in range(3)], axis=0)
    z = lax.dot_general(jnp.concatenate(data, axis=0), sea_weights, NT, preferred_element_type=F32)
    lane = lax.broadcasted_iota(jnp.int32, (rows, cols), 1)
    for o in range(n_sea):
        piece = lambda k, dc: z[k * rows : (k + 1) * rows, 16 * (dc + 1) + o : 16 * (dc + 1) + o + 1]
        extra = jnp.where(lane == 0, piece(0, -1) + piece(1, 0), 0.0)
        extra = jnp.where(lane == 1, piece(1, -1), extra)
        extra = jnp.where(lane == cols - 2, piece(2, 1), extra)
        extra = jnp.where(lane == cols - 1, piece(2, 0) + piece(3, 1), extra)
        v = (sea[o] + extra).astype(BF16).astype(F32)
        for b in range(n_blocks):
            blocks[b, o] = jnp.where(target[0:1] == b, v, 0.0).astype(BF16)


def rim_part(here, target, edges, far, near, conv_in, bias_in, conv_out, sea, n_blocks, n_sea):
    rows, cols = sea.shape[1:]
    chans = edges.shape[2]
    hid = conv_in.shape[1]
    return call(
        rim_kernel,
        [jax.ShapeDtypeStruct((4, LONG, hid), BF16), jax.ShapeDtypeStruct((n_blocks, n_sea, rows, cols), BF16)],
        [((8, LONG + 8, chans), F32), ((4, LONG, hid), F32)],
        (2 * 128 * 1152 * 256, 1500000, 128 * 256),
        10,
        here, target, edges, far, near, conv_in, bias_in, conv_out, sea,
    )


def out_kernel(hidden, rim, cells, conv_out, bias_out, new_state, z, flat):
    rows, cols, chans = cells.shape
    hid = hidden.shape[2]
    weights = conv_out[...].reshape(5 * chans, hid)
    step = 3
    for j in range(0, rows + 2, step):
        data = hidden[j : j + step].reshape(step * cols, hid)
        got = lax.dot_general(data, weights, NT, preferred_element_type=F32)
        z[j : j + step, 8 : 8 + cols] = got.reshape(step, cols, 5 * chans)
    got = lax.dot_general(rim[...].reshape(4 * LONG, hid), weights, NT, preferred_element_type=F32)
    for k, s in enumerate((7, 8, 7 + cols, 8 + cols)):
        for j in range(rows + 2):
            z[j, s : s + 1] = got[k * LONG + j : k * LONG + j + 1]
    cut = lambda j, t, s: z[j, 8 + s : 8 + s + cols, t * chans : (t + 1) * chans]
    for r in range(rows):
        j = r + 1
        total = cut(j, 0, 0) + cut(j - 1, 2, 0) + cut(j + 1, 2, 0)
        total += cut(j, 1, 1) + cut(j + 1, 3, 1) + cut(j - 1, 4, 1)
        total += cut(j, 1, -1) + cut(j - 1, 3, -1) + cut(j + 1, 4, -1)
        total += bias_out[...] + cells[r].astype(F32)
        flat[pl.ds(r, chans, stride=rows), :] = total.T
    new_state[...] = flat[...].reshape(chans, rows, cols).astype(BF16)


def out_part(hidden, rim, cells, conv_out, bias_out):
    rows, cols, chans = cells.shape
    return call(
        out_kernel,
        jax.ShapeDtypeStruct((chans, rows, cols), BF16),
        [((rows + 2, cols + 16, 5 * chans), F32), ((chans * rows, cols), F32)],
        (2 * 18 * 128 * 640 * 256, 3000000, 0),
        18,
        hidden, rim, cells, conv_out, bias_out,
    )


def sort_kernel(place, held, sent):
    count, chans, rows, cols = held.shape
    half = sent.shape[0] // 2
    named = [place[k] for k in range(count)]
    chosen = [[v == p for v in named] for p in range(half)]
    for o in range(chans):
        for i in range(0, rows, 16):
            parts = [held[k, o, i : i + 16].astype(F32) for k in range(count)]
            parts = [(v[:8], v[8:]) for v in parts]
            for p in range(half):
                total = [jnp.zeros((8, cols), F32)] * 2
                for k, v in enumerate(parts):
                    total = [jnp.where(chosen[p][k], x, t) for x, t in zip(v, total)]
                sent[p, o, i : i + 16] = jnp.concatenate(total).astype(BF16)
    sent[half:] = jnp.zeros((half,) + sent.shape[1:], BF16)


def sort_tiles(place, held, count):
    shape = jax.ShapeDtypeStruct((count,) + held.shape[1:], BF16)
    return call(sort_kernel, shape, [], (100000, 6 * held.size, 0), 6, place, held)


def exchange(values, partner):
    shape = tuple(lax.axis_size(a) for a in ALL)
    number = lambda f, r, c: (f * shape[1] + r) * shape[2] + c
    pairs = []
    for f in range(shape[0]):
        for r in range(shape[1]):
            for c in range(shape[2]):
                other = partner(f, r, c, shape)
                if other is not None:
                    pairs.append((number(f, r, c), number(*other)))
    return lax.ppermute(values, ALL, pairs)


def col_near(f, r, c, shape):
    return (f, r, c ^ 1)


def col_far(f, r, c, shape):
    if c == 0:
        return (f ^ 2, shape[1] - 1 - r, c)
    if c == shape[2] - 1:
        return (f ^ 1, shape[1] - 1 - r, c)
    return (f, r, ((c + 1) ^ 1) - 1)


def row_near(f, r, c, shape):
    return (f, r ^ 1, c)


def row_far(f, r, c, shape):
    return None if r in (0, shape[1] - 1) else (f, ((r + 1) ^ 1) - 1, c)


def local(state, conv_in, bias_in, conv_out, bias_out, land, owner):
    state = state[0]
    chans, height, width = state.shape
    rows, cols = lax.axis_size("row"), lax.axis_size("col")
    r, c = lax.axis_index("row"), lax.axis_index("col")
    lines = (r > 0, r < rows - 1, r, c, cols - 1, 0, 0, 0)
    here = jnp.concatenate([jnp.full((1, 128), v, jnp.int32) for v in lines])
    cells, edges, far, near, first = turn(here, state)

    far_rows, near_rows = exchange(far, row_far), exchange(near, row_near)

    tall, far, near = strips(here, edges, far_rows, near_rows)
    got_far = exchange(far, col_far)
    got_near = exchange(near, col_near)
    odd = c % 2 == 1
    got_near = jnp.concatenate([jnp.where(odd, got_near, 0), jnp.where(odd, 0, got_near)])

    target, place = routes(jnp.concatenate([owner, land]), here)
    bias_in, bias_out = bias_in[None], bias_out[None]
    wide = cells.astype(F32)
    hidden, sea = inner_part(here, wide, far_rows, near_rows, conv_in, bias_in, conv_out, bias_out, first)
    rim, blocks = rim_part(here, target, tall, got_far, got_near, conv_in, bias_in, conv_out, sea, cols, OC)
    held = lax.all_to_all(blocks, "col", 0, 0, tiled=True)
    new_state = out_part(hidden, rim, cells, conv_out, bias_out)
    sent = sort_tiles(place, held, rows * CAP).reshape((rows, CAP, OC, height, width))
    got = lax.all_to_all(sent, "row", 0, 0, tiled=True)
    ocean = jnp.sum(got.astype(F32), axis=0).astype(BF16)
    return (new_state[None], ocean[None, None])


def solution(mesh):
    in_specs = (P("face", None, "row", "col"), P(), P(), P(), P(), P("face", None), P("face", None))
    out_specs = (P("face", None, "row", "col"), P("face", ("row", "col"), None, None, None, None))
    return jax.shard_map(local, mesh=mesh, in_specs=in_specs, out_specs=out_specs, check_vma=False)
```

```python
import jax
import jax.numpy as jnp
from jax import lax
from jax.experimental import pallas as pl
from jax.experimental.pallas import tpu as pltpu
from jax.sharding import PartitionSpec as P

OC = 4
CAP = 2
ALL = ("face", "row", "col")
BORDER = 2
LONG = 32
SHARE = 6
OWNER_AT, LAND_AT, IN_AT, OUT_AT = 0, 128, 256, 512
TAPS = (3, 2, 4, 1, 0, 1, 4, 2, 3)
NT = (((1,), (1,)), ((), ()))
VM = pl.BlockSpec(memory_space=pltpu.VMEM)
F32 = jnp.float32
BF16 = jnp.bfloat16


def call(kernel, out_shape, scratch, cost, room, *operands):
    many = isinstance(out_shape, list)
    return pl.pallas_call(
        kernel,
        out_shape=out_shape,
        in_specs=[VM] * len(operands),
        out_specs=[VM] * len(out_shape) if many else VM,
        scratch_shapes=[pltpu.VMEM(s, d) for s, d in scratch],
        compiler_params=pltpu.CompilerParams(vmem_limit_bytes=room * 2**20),
        cost_estimate=pl.CostEstimate(flops=cost[0], bytes_accessed=cost[1], transcendentals=cost[2]),
    )(*operands)


def turn_kernel(here, state, turned, edges, far, near, first, flat):
    chans, rows, cols = state.shape
    flat[...] = state[...].reshape(chans * rows, cols).astype(F32)
    for r in range(rows):
        turned[r] = flat[pl.ds(r, chans, stride=rows), :].T
    for k, w in enumerate((0, 1, cols - 2, cols - 1)):
        edges[k] = turned.reshape(rows * cols, chans)[pl.ds(w, rows, stride=cols), :].astype(BF16)
    odd = jnp.broadcast_to((here[2:3] & 1) == 1, (cols, chans))
    ends = (0, 1, cols - 2, cols - 1)
    lines = lambda r: [turned[r + k, w : w + 1] for w in ends for k in range(BORDER)]
    rest = jnp.zeros((8, chans), F32)
    top, bottom = (jnp.concatenate(lines(r) + [rest]) for r in (0, rows - BORDER))
    far[BORDER * cols :] = jnp.where(odd[:16], bottom, top).astype(BF16)
    near[BORDER * cols :] = jnp.where(odd[:16], top, bottom).astype(BF16)
    for k in range(BORDER):
        top, bottom = turned[k], turned[rows - BORDER + k]
        far[k * cols : (k + 1) * cols] = jnp.where(odd, bottom, top).astype(BF16)
        near[k * cols : (k + 1) * cols] = jnp.where(odd, top, bottom).astype(BF16)
    first[...] = state[0:8].astype(F32)


def turn(here, state):
    chans, rows, cols = state.shape
    strip = jax.ShapeDtypeStruct((BORDER * cols + 16, chans), BF16)
    return call(
        turn_kernel,
        [jax.ShapeDtypeStruct((rows, cols, chans), F32), jax.ShapeDtypeStruct((4, rows, chans), BF16), strip, strip]
        + [jax.ShapeDtypeStruct((8, rows, cols), F32)],
        [((chans * rows, cols), F32)],
        (0, 4 * state.size, 0),
        10,
        here,
        state,
    )


def route_kernel(pack, here, target, place):
    count = 64
    cols = rows = 8
    wide = lambda v: jnp.broadcast_to(v, (count, count))
    i = lax.broadcasted_iota(jnp.int32, (count, count), 0)
    j = lax.broadcasted_iota(jnp.int32, (count, count), 1)
    own, land = (pack[:, at : at + count].astype(jnp.int32) for at in (OWNER_AT, LAND_AT))
    own, wet = wide(own), wide(1 - land)
    down = lambda v: jnp.sum(jnp.where(i == j, v, 0).astype(F32), axis=1, keepdims=True)
    own_i, wet_i = down(own), down(wet)
    same = (own.astype(F32) == own_i) & (wet == 1) & (j < i)
    slot = jnp.sum(jnp.where(same, 1.0, 0.0), axis=1, keepdims=True)
    lanes = here.shape[1]
    spread = lambda v: jnp.broadcast_to(v, (count, lanes))
    own_i, wet_i, slot = spread(own_i).astype(jnp.int32), spread(wet_i), spread(slot).astype(jnp.int32)
    tile = lax.broadcasted_iota(jnp.int32, (count, lanes), 0)
    r, c = here[2:3], here[3:4]
    mine = (tile == r * cols + c) & (wet_i > 0)
    to_col = jnp.sum(jnp.where(mine, (own_i & (cols - 1)) + 1, 0).astype(F32), axis=0, keepdims=True) - 1.0
    target[...] = jnp.broadcast_to(to_col, target.shape)
    spot = jnp.where((wet_i > 0) & ((own_i & (cols - 1)) == c), (own_i >> 3) * 2 + slot, -1).astype(F32)
    total = jnp.full((cols, lanes), 0.0, F32)
    for k in range(rows):
        total = jnp.where(r == k, spot[k * cols : (k + 1) * cols], total)
    for k in range(cols):
        place[k] = jnp.broadcast_to(total[k : k + 1], place.shape[1:])


def routes(pack, here):
    lanes = here.shape[1]
    shapes = [jax.ShapeDtypeStruct((8, lanes), F32), jax.ShapeDtypeStruct((8, 8, lanes), F32)]
    return call(route_kernel, shapes, [], (100000, 50000, 0), 4, pack, here)


def strip_kernel(here, edges, got_far, got_near, tall, far, near, field, picked):
    count, rows, chans = edges.shape
    length = rows + 2 * BORDER
    odd_row = jnp.broadcast_to((here[2:3] & 1) == 1, (16, chans))
    tail = got_far.shape[0] - 16
    a, b = got_far[tail:].astype(F32), got_near[tail:].astype(F32)
    above, below = jnp.where(odd_row, b, a), jnp.where(odd_row, a, b)
    for k in range(count):
        field[k, 0:BORDER] = above[BORDER * k : BORDER * (k + 1)]
        field[k, BORDER : BORDER + rows] = edges[k].astype(F32)
        field[k, BORDER + rows : length] = below[BORDER * k : BORDER * (k + 1)]
        field[k, length:] = jnp.zeros((field.shape[1] - length, chans), F32)
        tall[k] = field[k].astype(BF16)
    col = jnp.broadcast_to(here[3:4], (LONG, chans))
    odd = (col & 1) == 1
    seam = (col == 0) | (col == here[4:5])
    for k in range(BORDER):
        west, east = field[k], field[BORDER + k]
        near[k] = jnp.where(odd, west, east).astype(BF16)
        picked[k] = jnp.where(odd, east, west)
    for k in range(BORDER):
        for r in range(length):
            field[k, r : r + 1] = picked[BORDER - 1 - k, length - 1 - r : length - r]
    for k in range(BORDER):
        far[k] = jnp.where(seam, field[k], picked[k]).astype(BF16)


def strips(here, edges, got_far, got_near):
    count, rows, chans = edges.shape
    two = jax.ShapeDtypeStruct((BORDER, LONG, chans), BF16)
    return call(
        strip_kernel,
        [jax.ShapeDtypeStruct((count, LONG, chans), BF16), two, two],
        [((count, LONG, chans), F32), ((BORDER, LONG, chans), F32)],
        (0, 200000, 0),
        4,
        here, edges, got_far, got_near,
    )


def inner_kernel(here, cells, got_far, got_near, conv_in, pack, conv_out, first, *refs):
    *hidden, sea, field, taps = refs
    rows, cols, chans = cells.shape
    hid = conv_in.shape[1]
    bias_in = pack[:, IN_AT : IN_AT + hid]
    for r in range(rows):
        field[BORDER + r, 8 : 8 + cols] = cells[r].astype(F32)
    odd = jnp.broadcast_to((here[2:3] & 1) == 1, (cols, chans))
    for k in range(BORDER):
        far, near = (v[k * cols : (k + 1) * cols].astype(F32) for v in (got_far, got_near))
        field[k, 8 : 8 + cols] = jnp.where(odd, near, far)
        field[BORDER + rows + k, 8 : 8 + cols] = jnp.where(odd, far, near)
    for r in range(rows + 2 * BORDER):
        for k in range(3):
            taps[r, :, k * chans : (k + 1) * chans] = field[r, 7 + k : 7 + k + cols].astype(BF16)
    weights = jnp.concatenate([conv_in[t] for t in TAPS], axis=1)
    col = lax.broadcasted_iota(jnp.int32, (cols, hid), 0)
    inside = (col > 0) & (col < cols - 1)
    keep = jnp.concatenate([here[0:2]] * (hid // here.shape[1]), axis=1) > 0
    step = 3
    for j in range(0, rows + 2, step):
        data = jnp.concatenate([taps[j + d : j + d + step].reshape(step * cols, 3 * chans) for d in range(3)], axis=1)
        x = lax.dot_general(data, weights, NT, preferred_element_type=F32) + bias_in
        x = jax.nn.gelu(x).reshape(step, cols, hid)
        for d in range(step):
            here_in = inside
            if j + d == 0:
                here_in = inside & keep[0:1]
            if j + d == rows + 1:
                here_in = inside & keep[1:2]
            hidden[(j + d) // SHARE][(j + d) % SHARE] = jnp.where(here_in, x[d], 0.0).astype(BF16)
    sea_weights = conv_out[:, 0:16].reshape(5 * 16, hid)
    z = []
    for j in range(0, rows + 2, 2):
        two = lax.dot_general(sea_weights, hidden[j // SHARE][j % SHARE : j % SHARE + 2].reshape(2 * cols, hid), NT, preferred_element_type=F32)
        z += [two[:, :cols], two[:, cols:]]
    cut = lambda j, t: z[j][16 * t : 16 * t + 8]
    upper = pack[:, OUT_AT : OUT_AT + chans]
    lane = lax.broadcasted_iota(jnp.int32, (8, upper.shape[1]), 1)
    channel = lax.broadcasted_iota(jnp.int32, (8, upper.shape[1]), 0)
    bias_sea = jnp.sum(jnp.where(lane == channel, upper, 0.0), axis=1, keepdims=True)
    for r in range(rows):
        j = r + 1
        mid = cut(j, 0) + cut(j - 1, 2) + cut(j + 1, 2)
        plus = cut(j, 1) + cut(j + 1, 3) + cut(j - 1, 4)
        minus = cut(j, 1) + cut(j - 1, 3) + cut(j + 1, 4)
        total = mid + pltpu.roll(plus, cols - 1, 1) + pltpu.roll(minus, 1, 1) + bias_sea
        sea[:, r] = total
    sea[...] += first[...]


def inner_part(here, cells, got_far, got_near, conv_in, pack, conv_out, first):
    rows, cols, chans = cells.shape
    hid = conv_in.shape[1]
    return call(
        inner_kernel,
        [jax.ShapeDtypeStruct((SHARE, cols, hid), BF16)] * ((rows + 2) // SHARE)
        + [jax.ShapeDtypeStruct((8, rows, cols), F32)],
        [((rows + 4, cols + 16, chans), F32), ((rows + 4, cols, 3 * chans), BF16)],
        (2 * 18 * 128 * (1152 + 80) * 256, 3000000, 18 * 128 * 256),
        14,
        here, cells, got_far, got_near, conv_in, pack, conv_out, first,
    )


def rim_kernel(here, target, edges, far, near, conv_in, pack, conv_out, sea, rim, blocks, field, tall):
    hid = conv_in.shape[1]
    bias_in = pack[:, IN_AT : IN_AT + hid]
    n_blocks, n_sea, rows, cols = blocks.shape
    odd = jnp.broadcast_to((here[3:4] & 1) == 1, (LONG, field.shape[2]))
    for k, w in enumerate((-1, -1, 0, 1, 2, 3, -1, -1)):
        if w >= 0:
            field[k, 0:LONG] = edges[w].astype(F32)
        else:
            i, j = (k, k) if k < 2 else (k - 6, k - 4)
            one, two = far[i].astype(F32), near[j].astype(F32)
            field[k, 0:LONG] = jnp.where(odd, two, one) if k < 2 else jnp.where(odd, one, two)
        field[k, LONG : LONG + 8] = jnp.zeros((8, field.shape[2]), F32)
    weights = jnp.concatenate([conv_in[t] for t in TAPS], axis=1)
    data = []
    for k in (1, 2, 5, 6):
        data.append(jnp.concatenate([field[k + dc, dr : dr + LONG].astype(BF16) for dr in range(3) for dc in (-1, 0, 1)], axis=1))
    x = lax.dot_general(jnp.concatenate(data, axis=0), weights, NT, preferred_element_type=F32) + bias_in
    x = jax.nn.gelu(x)
    keep = jnp.concatenate([here[0:2]] * (hid // here.shape[1]), axis=1) > 0
    row = lax.broadcasted_iota(jnp.int32, (LONG, hid), 0)
    inside = ((row > 0) | keep[0:1]) & ((row < rows + 1) | keep[1:2]) & (row < rows + 2)
    for k in range(4):
        tall[k] = jnp.where(inside, x[k * LONG : (k + 1) * LONG], 0.0).astype(BF16).astype(F32)
        rim[k] = tall[k].astype(BF16)
    data = [jnp.concatenate([tall[k, d : d + rows].astype(BF16) for d in range(3)], axis=1) for k in range(4)]
    part = lambda dc: jnp.concatenate([conv_out[TAPS[3 * dr + dc], 0:16] for dr in range(3)], axis=1)
    sea_weights = jnp.concatenate([part(dc) for dc in range(3)], axis=0)
    z = lax.dot_general(jnp.concatenate(data, axis=0), sea_weights, NT, preferred_element_type=F32)
    lane = lax.broadcasted_iota(jnp.int32, (rows, cols), 1)
    for o in range(n_sea):
        piece = lambda k, dc: z[k * rows : (k + 1) * rows, 16 * (dc + 1) + o : 16 * (dc + 1) + o + 1]
        extra = jnp.where(lane == 0, piece(0, -1) + piece(1, 0), 0.0)
        extra = jnp.where(lane == 1, piece(1, -1), extra)
        extra = jnp.where(lane == cols - 2, piece(2, 1), extra)
        extra = jnp.where(lane == cols - 1, piece(2, 0) + piece(3, 1), extra)
        v = (sea[o] + extra).astype(BF16).astype(F32)
        for b in range(n_blocks):
            blocks[b, o] = jnp.where(target[0:1] == b, v, 0.0).astype(BF16)


def rim_part(here, target, edges, far, near, conv_in, pack, conv_out, sea, n_blocks, n_sea):
    rows, cols = sea.shape[1:]
    chans = edges.shape[2]
    hid = conv_in.shape[1]
    return call(
        rim_kernel,
        [jax.ShapeDtypeStruct((4, LONG, hid), BF16), jax.ShapeDtypeStruct((n_blocks, n_sea, rows, cols), BF16)],
        [((8, LONG + 8, chans), F32), ((4, LONG, hid), F32)],
        (2 * 128 * 1152 * 256, 1500000, 128 * 256),
        10,
        here, target, edges, far, near, conv_in, pack, conv_out, sea,
    )


def out_kernel(*refs):
    *hidden, rim, cells, conv_out, pack, new_state, done, z, flat = refs
    rows, cols, chans = cells.shape
    hid = rim.shape[2]
    weights = conv_out[...].reshape(5 * chans, hid)
    step = 3
    for j in range(0, rows + 2, step):
        data = hidden[j // SHARE][j % SHARE : j % SHARE + step].reshape(step * cols, hid)
        got = lax.dot_general(data, weights, NT, preferred_element_type=F32)
        z[j : j + step, 8 : 8 + cols] = got.reshape(step, cols, 5 * chans)
    got = lax.dot_general(rim[...].reshape(4 * LONG, hid), weights, NT, preferred_element_type=F32)
    for k, s in enumerate((7, 8, 7 + cols, 8 + cols)):
        for j in range(rows + 2):
            z[j, s : s + 1] = got[k * LONG + j : k * LONG + j + 1]
    cut = lambda j, t, s: z[j, 8 + s : 8 + s + cols, t * chans : (t + 1) * chans]
    for r in range(rows):
        j = r + 1
        total = cut(j, 0, 0) + cut(j - 1, 2, 0) + cut(j + 1, 2, 0)
        total += cut(j, 1, 1) + cut(j + 1, 3, 1) + cut(j - 1, 4, 1)
        total += cut(j, 1, -1) + cut(j - 1, 3, -1) + cut(j + 1, 4, -1)
        total += pack[:, OUT_AT : OUT_AT + chans] + cells[r].astype(F32)
        flat[pl.ds(r, chans, stride=rows), :] = total.T
    new_state[...] = flat[...].reshape(chans, rows, cols).astype(BF16)
    done[...] = jnp.zeros_like(done)


def out_part(hidden, rim, cells, conv_out, pack):
    rows, cols, chans = cells.shape
    return call(
        out_kernel,
        [jax.ShapeDtypeStruct((chans, rows, cols), BF16), jax.ShapeDtypeStruct((8, cols), F32)],
        [((rows + 2, cols + 16, 5 * chans), F32), ((chans * rows, cols), F32)],
        (2 * 18 * 128 * 640 * 256, 3000000, 0),
        18,
        *hidden, rim, cells, conv_out, pack,
    )


def sort_kernel(place, held, done, sent):
    count, chans, rows, cols = held.shape
    half = sent.shape[0] // 2
    named = [place[k] for k in range(count)]
    chosen = [[v == p for v in named] for p in range(half)]
    for o in range(chans):
        for i in range(0, rows, 16):
            parts = [held[k, o, i : i + 16].astype(F32) for k in range(count)]
            parts = [(v[:8], v[8:]) for v in parts]
            for p in range(half):
                total = [jnp.zeros((8, cols), F32)] * 2
                for k, v in enumerate(parts):
                    total = [jnp.where(chosen[p][k], x, t) for x, t in zip(v, total)]
                sent[p, o, i : i + 16] = jnp.concatenate(total).astype(BF16)
    sent[half:] = jnp.zeros((half,) + sent.shape[1:], BF16)


def sort_tiles(place, held, done, count):
    shape = jax.ShapeDtypeStruct((count,) + held.shape[1:], BF16)
    return call(sort_kernel, shape, [], (100000, 6 * held.size, 0), 6, place, held, done)


def exchange(values, partner):
    shape = tuple(lax.axis_size(a) for a in ALL)
    number = lambda f, r, c: (f * shape[1] + r) * shape[2] + c
    pairs = []
    for f in range(shape[0]):
        for r in range(shape[1]):
            for c in range(shape[2]):
                other = partner(f, r, c, shape)
                if other is not None:
                    pairs.append((number(f, r, c), number(*other)))
    return lax.ppermute(values, ALL, pairs)


def col_near(f, r, c, shape):
    return (f, r, c ^ 1)


def col_far(f, r, c, shape):
    if c == 0:
        return (f ^ 2, shape[1] - 1 - r, c)
    if c == shape[2] - 1:
        return (f ^ 1, shape[1] - 1 - r, c)
    return (f, r, ((c + 1) ^ 1) - 1)


def row_near(f, r, c, shape):
    return (f, r ^ 1, c)


def row_far(f, r, c, shape):
    return None if r in (0, shape[1] - 1) else (f, ((r + 1) ^ 1) - 1, c)


def local(state, conv_in, bias_in, conv_out, bias_out, land, owner):
    state = state[0]
    chans, height, width = state.shape
    rows, cols = lax.axis_size("row"), lax.axis_size("col")
    r, c = lax.axis_index("row"), lax.axis_index("col")
    lines = (r > 0, r < rows - 1, r, c, cols - 1, 0, 0, 0)
    here = jnp.concatenate([jnp.full((1, 128), v, jnp.int32) for v in lines])
    cells, edges, far, near, first = turn(here, state)

    far_rows, near_rows = exchange(far, row_far), exchange(near, row_near)

    tall, far, near = strips(here, edges, far_rows, near_rows)
    got_far = exchange(far, col_far)
    got_near = exchange(near, col_near)
    odd = c % 2 == 1
    got_near = jnp.concatenate([jnp.where(odd, got_near, 0), jnp.where(odd, 0, got_near)])

    lane = lambda v: jnp.pad(v.astype(F32), ((0, 0), (0, 128 - v.shape[1])))
    pack = jnp.concatenate([lane(owner), lane(land), bias_in[None], bias_out[None]], axis=1)
    target, place = routes(pack, here)
    cells = cells.astype(BF16)
    *hidden, sea = inner_part(here, cells, far_rows, near_rows, conv_in, pack, conv_out, first)
    rim, blocks = rim_part(here, target, tall, got_far, got_near, conv_in, pack, conv_out, sea, cols, OC)
    held = lax.all_to_all(blocks, "col", 0, 0, tiled=True)
    new_state, done = out_part(hidden, rim, cells, conv_out, pack)
    sent = sort_tiles(place, held, done, rows * CAP).reshape((rows, CAP, OC, height, width))
    got = lax.all_to_all(sent, "row", 0, 0, tiled=True)
    ocean = jnp.sum(got.astype(F32), axis=0).astype(BF16)
    return (new_state[None], ocean[None, None])


def solution(mesh):
    in_specs = (P("face", None, "row", "col"), P(), P(), P(), P(), P("face", None), P("face", None))
    out_specs = (P("face", None, "row", "col"), P("face", ("row", "col"), None, None, None, None))
    return jax.shard_map(local, mesh=mesh, in_specs=in_specs, out_specs=out_specs, check_vma=False)
```

```python
import jax
import jax.numpy as jnp
from jax import lax
from jax.experimental import pallas as pl
from jax.experimental.pallas import tpu as pltpu
from jax.sharding import PartitionSpec as P

OC = 4
CAP = 2
ALL = ("face", "row", "col")
BORDER = 2
LONG = 32
SHARE = 6
OWNER_AT, LAND_AT, IN_AT, OUT_AT = 0, 128, 256, 512
TAPS = (3, 2, 4, 1, 0, 1, 4, 2, 3)
NT = (((1,), (1,)), ((), ()))
VM = pl.BlockSpec(memory_space=pltpu.VMEM)
F32 = jnp.float32
BF16 = jnp.bfloat16


def call(kernel, out_shape, scratch, cost, room, *operands):
    many = isinstance(out_shape, list)
    return pl.pallas_call(
        kernel,
        out_shape=out_shape,
        in_specs=[VM] * len(operands),
        out_specs=[VM] * len(out_shape) if many else VM,
        scratch_shapes=[pltpu.VMEM(s, d) for s, d in scratch],
        compiler_params=pltpu.CompilerParams(vmem_limit_bytes=room * 2**20),
        cost_estimate=pl.CostEstimate(flops=cost[0], bytes_accessed=cost[1], transcendentals=cost[2]),
    )(*operands)


def turn_kernel(here, state, turned, edges, far, near, first, flat):
    chans, rows, cols = state.shape
    flat[...] = state[...].reshape(chans * rows, cols).astype(F32)
    for r in range(rows):
        turned[r] = flat[pl.ds(r, chans, stride=rows), :].T
    for k, w in enumerate((0, 1, cols - 2, cols - 1)):
        edges[k] = turned.reshape(rows * cols, chans)[pl.ds(w, rows, stride=cols), :].astype(BF16)
    odd = jnp.broadcast_to((here[2:3] & 1) == 1, (cols, chans))
    ends = (0, 1, cols - 2, cols - 1)
    lines = lambda r: [turned[r + k, w : w + 1] for w in ends for k in range(BORDER)]
    rest = jnp.zeros((8, chans), F32)
    top, bottom = (jnp.concatenate(lines(r) + [rest]) for r in (0, rows - BORDER))
    far[BORDER * cols :] = jnp.where(odd[:16], bottom, top).astype(BF16)
    near[BORDER * cols :] = jnp.where(odd[:16], top, bottom).astype(BF16)
    for k in range(BORDER):
        top, bottom = turned[k], turned[rows - BORDER + k]
        far[k * cols : (k + 1) * cols] = jnp.where(odd, bottom, top).astype(BF16)
        near[k * cols : (k + 1) * cols] = jnp.where(odd, top, bottom).astype(BF16)
    first[...] = state[0:8].astype(F32)


def turn(here, state):
    chans, rows, cols = state.shape
    strip = jax.ShapeDtypeStruct((BORDER * cols + 16, chans), BF16)
    return call(
        turn_kernel,
        [jax.ShapeDtypeStruct((rows, cols, chans), F32), jax.ShapeDtypeStruct((4, rows, chans), BF16), strip, strip]
        + [jax.ShapeDtypeStruct((8, rows, cols), F32)],
        [((chans * rows, cols), F32)],
        (0, 4 * state.size, 0),
        10,
        here,
        state,
    )


def route_kernel(pack, here, target, place):
    count = 64
    cols = rows = 8
    wide = lambda v: jnp.broadcast_to(v, (count, count))
    i = lax.broadcasted_iota(jnp.int32, (count, count), 0)
    j = lax.broadcasted_iota(jnp.int32, (count, count), 1)
    own, land = (pack[:, at : at + count].astype(jnp.int32) for at in (OWNER_AT, LAND_AT))
    own, wet = wide(own), wide(1 - land)
    down = lambda v: jnp.sum(jnp.where(i == j, v, 0).astype(F32), axis=1, keepdims=True)
    own_i, wet_i = down(own), down(wet)
    same = (own.astype(F32) == own_i) & (wet == 1) & (j < i)
    slot = jnp.sum(jnp.where(same, 1.0, 0.0), axis=1, keepdims=True)
    lanes = here.shape[1]
    spread = lambda v: jnp.broadcast_to(v, (count, lanes))
    own_i, wet_i, slot = spread(own_i).astype(jnp.int32), spread(wet_i), spread(slot).astype(jnp.int32)
    tile = lax.broadcasted_iota(jnp.int32, (count, lanes), 0)
    r, c = here[2:3], here[3:4]
    mine = (tile == r * cols + c) & (wet_i > 0)
    to_row = jnp.sum(jnp.where(mine, (own_i >> 3) + 1, 0).astype(F32), axis=0, keepdims=True) - 1.0
    target[...] = jnp.broadcast_to(to_row, target.shape)
    held = (wet_i > 0) & ((own_i >> 3) == r) & ((tile & (cols - 1)) == c)
    spot = jnp.where(held, (own_i & (cols - 1)) * 2 + slot + 1, 0).astype(F32)
    total = jnp.sum(spot.reshape(rows, cols, lanes), axis=1) - 1.0
    for k in range(cols):
        place[k] = jnp.broadcast_to(total[k : k + 1], place.shape[1:])


def routes(pack, here):
    lanes = here.shape[1]
    shapes = [jax.ShapeDtypeStruct((8, lanes), F32), jax.ShapeDtypeStruct((8, 8, lanes), F32)]
    return call(route_kernel, shapes, [], (100000, 50000, 0), 4, pack, here)


def strip_kernel(here, edges, got_far, got_near, tall, far, near, field, picked):
    count, rows, chans = edges.shape
    length = rows + 2 * BORDER
    odd_row = jnp.broadcast_to((here[2:3] & 1) == 1, (16, chans))
    tail = got_far.shape[0] - 16
    a, b = got_far[tail:].astype(F32), got_near[tail:].astype(F32)
    above, below = jnp.where(odd_row, b, a), jnp.where(odd_row, a, b)
    for k in range(count):
        field[k, 0:BORDER] = above[BORDER * k : BORDER * (k + 1)]
        field[k, BORDER : BORDER + rows] = edges[k].astype(F32)
        field[k, BORDER + rows : length] = below[BORDER * k : BORDER * (k + 1)]
        field[k, length:] = jnp.zeros((field.shape[1] - length, chans), F32)
        tall[k] = field[k].astype(BF16)
    col = jnp.broadcast_to(here[3:4], (LONG, chans))
    odd = (col & 1) == 1
    seam = (col == 0) | (col == here[4:5])
    for k in range(BORDER):
        west, east = field[k], field[BORDER + k]
        near[k] = jnp.where(odd, west, east).astype(BF16)
        picked[k] = jnp.where(odd, east, west)
    for k in range(BORDER):
        for r in range(length):
            field[k, r : r + 1] = picked[BORDER - 1 - k, length - 1 - r : length - r]
    for k in range(BORDER):
        far[k] = jnp.where(seam, field[k], picked[k]).astype(BF16)


def strips(here, edges, got_far, got_near):
    count, rows, chans = edges.shape
    two = jax.ShapeDtypeStruct((BORDER, LONG, chans), BF16)
    return call(
        strip_kernel,
        [jax.ShapeDtypeStruct((count, LONG, chans), BF16), two, two],
        [((count, LONG, chans), F32), ((BORDER, LONG, chans), F32)],
        (0, 200000, 0),
        4,
        here, edges, got_far, got_near,
    )


def inner_kernel(here, cells, got_far, got_near, conv_in, pack, conv_out, first, *refs):
    *hidden, sea, field, taps = refs
    rows, cols, chans = cells.shape
    hid = conv_in.shape[1]
    bias_in = pack[:, IN_AT : IN_AT + hid]
    for r in range(rows):
        field[BORDER + r, 8 : 8 + cols] = cells[r].astype(F32)
    odd = jnp.broadcast_to((here[2:3] & 1) == 1, (cols, chans))
    for k in range(BORDER):
        far, near = (v[k * cols : (k + 1) * cols].astype(F32) for v in (got_far, got_near))
        field[k, 8 : 8 + cols] = jnp.where(odd, near, far)
        field[BORDER + rows + k, 8 : 8 + cols] = jnp.where(odd, far, near)
    for r in range(rows + 2 * BORDER):
        for k in range(3):
            taps[r, :, k * chans : (k + 1) * chans] = field[r, 7 + k : 7 + k + cols].astype(BF16)
    weights = jnp.concatenate([conv_in[t] for t in TAPS], axis=1)
    col = lax.broadcasted_iota(jnp.int32, (cols, hid), 0)
    inside = (col > 0) & (col < cols - 1)
    keep = jnp.concatenate([here[0:2]] * (hid // here.shape[1]), axis=1) > 0
    step = 3
    for j in range(0, rows + 2, step):
        data = jnp.concatenate([taps[j + d : j + d + step].reshape(step * cols, 3 * chans) for d in range(3)], axis=1)
        x = lax.dot_general(data, weights, NT, preferred_element_type=F32) + bias_in
        x = jax.nn.gelu(x).reshape(step, cols, hid)
        for d in range(step):
            here_in = inside
            if j + d == 0:
                here_in = inside & keep[0:1]
            if j + d == rows + 1:
                here_in = inside & keep[1:2]
            hidden[(j + d) // SHARE][(j + d) % SHARE] = jnp.where(here_in, x[d], 0.0).astype(BF16)
    sea_weights = conv_out[:, 0:16].reshape(5 * 16, hid)
    z = []
    for j in range(0, rows + 2, 2):
        two = lax.dot_general(sea_weights, hidden[j // SHARE][j % SHARE : j % SHARE + 2].reshape(2 * cols, hid), NT, preferred_element_type=F32)
        z += [two[:, :cols], two[:, cols:]]
    cut = lambda j, t: z[j][16 * t : 16 * t + 8]
    upper = pack[:, OUT_AT : OUT_AT + chans]
    lane = lax.broadcasted_iota(jnp.int32, (8, upper.shape[1]), 1)
    channel = lax.broadcasted_iota(jnp.int32, (8, upper.shape[1]), 0)
    bias_sea = jnp.sum(jnp.where(lane == channel, upper, 0.0), axis=1, keepdims=True)
    for r in range(rows):
        j = r + 1
        mid = cut(j, 0) + cut(j - 1, 2) + cut(j + 1, 2)
        plus = cut(j, 1) + cut(j + 1, 3) + cut(j - 1, 4)
        minus = cut(j, 1) + cut(j - 1, 3) + cut(j + 1, 4)
        total = mid + pltpu.roll(plus, cols - 1, 1) + pltpu.roll(minus, 1, 1) + bias_sea
        sea[:, r] = total
    sea[...] += first[...]


def inner_part(here, cells, got_far, got_near, conv_in, pack, conv_out, first):
    rows, cols, chans = cells.shape
    hid = conv_in.shape[1]
    return call(
        inner_kernel,
        [jax.ShapeDtypeStruct((SHARE, cols, hid), BF16)] * ((rows + 2) // SHARE)
        + [jax.ShapeDtypeStruct((8, rows, cols), F32)],
        [((rows + 4, cols + 16, chans), F32), ((rows + 4, cols, 3 * chans), BF16)],
        (2 * 18 * 128 * (1152 + 80) * 256, 3000000, 18 * 128 * 256),
        14,
        here, cells, got_far, got_near, conv_in, pack, conv_out, first,
    )


def rim_kernel(here, target, edges, far, near, conv_in, pack, conv_out, sea, rim, blocks, field, tall):
    hid = conv_in.shape[1]
    bias_in = pack[:, IN_AT : IN_AT + hid]
    n_blocks, n_sea, rows, cols = blocks.shape
    odd = jnp.broadcast_to((here[3:4] & 1) == 1, (LONG, field.shape[2]))
    for k, w in enumerate((-1, -1, 0, 1, 2, 3, -1, -1)):
        if w >= 0:
            field[k, 0:LONG] = edges[w].astype(F32)
        else:
            i, j = (k, k) if k < 2 else (k - 6, k - 4)
            one, two = far[i].astype(F32), near[j].astype(F32)
            field[k, 0:LONG] = jnp.where(odd, two, one) if k < 2 else jnp.where(odd, one, two)
        field[k, LONG : LONG + 8] = jnp.zeros((8, field.shape[2]), F32)
    weights = jnp.concatenate([conv_in[t] for t in TAPS], axis=1)
    data = []
    for k in (1, 2, 5, 6):
        data.append(jnp.concatenate([field[k + dc, dr : dr + LONG].astype(BF16) for dr in range(3) for dc in (-1, 0, 1)], axis=1))
    x = lax.dot_general(jnp.concatenate(data, axis=0), weights, NT, preferred_element_type=F32) + bias_in
    x = jax.nn.gelu(x)
    keep = jnp.concatenate([here[0:2]] * (hid // here.shape[1]), axis=1) > 0
    row = lax.broadcasted_iota(jnp.int32, (LONG, hid), 0)
    inside = ((row > 0) | keep[0:1]) & ((row < rows + 1) | keep[1:2]) & (row < rows + 2)
    for k in range(4):
        tall[k] = jnp.where(inside, x[k * LONG : (k + 1) * LONG], 0.0).astype(BF16).astype(F32)
        rim[k] = tall[k].astype(BF16)
    data = [jnp.concatenate([tall[k, d : d + rows].astype(BF16) for d in range(3)], axis=1) for k in range(4)]
    part = lambda dc: jnp.concatenate([conv_out[TAPS[3 * dr + dc], 0:16] for dr in range(3)], axis=1)
    sea_weights = jnp.concatenate([part(dc) for dc in range(3)], axis=0)
    z = lax.dot_general(jnp.concatenate(data, axis=0), sea_weights, NT, preferred_element_type=F32)
    lane = lax.broadcasted_iota(jnp.int32, (rows, cols), 1)
    for o in range(n_sea):
        piece = lambda k, dc: z[k * rows : (k + 1) * rows, 16 * (dc + 1) + o : 16 * (dc + 1) + o + 1]
        extra = jnp.where(lane == 0, piece(0, -1) + piece(1, 0), 0.0)
        extra = jnp.where(lane == 1, piece(1, -1), extra)
        extra = jnp.where(lane == cols - 2, piece(2, 1), extra)
        extra = jnp.where(lane == cols - 1, piece(2, 0) + piece(3, 1), extra)
        v = (sea[o] + extra).astype(BF16).astype(F32)
        for b in range(n_blocks):
            blocks[b, o] = jnp.where(target[0:1] == b, v, 0.0).astype(BF16)


def rim_part(here, target, edges, far, near, conv_in, pack, conv_out, sea, n_blocks, n_sea):
    rows, cols = sea.shape[1:]
    chans = edges.shape[2]
    hid = conv_in.shape[1]
    return call(
        rim_kernel,
        [jax.ShapeDtypeStruct((4, LONG, hid), BF16), jax.ShapeDtypeStruct((n_blocks, n_sea, rows, cols), BF16)],
        [((8, LONG + 8, chans), F32), ((4, LONG, hid), F32)],
        (2 * 128 * 1152 * 256, 1500000, 128 * 256),
        10,
        here, target, edges, far, near, conv_in, pack, conv_out, sea,
    )


def out_kernel(*refs):
    *hidden, rim, cells, conv_out, pack, new_state, done, z, flat = refs
    rows, cols, chans = cells.shape
    hid = rim.shape[2]
    weights = conv_out[...].reshape(5 * chans, hid)
    step = 3
    for j in range(0, rows + 2, step):
        data = hidden[j // SHARE][j % SHARE : j % SHARE + step].reshape(step * cols, hid)
        got = lax.dot_general(data, weights, NT, preferred_element_type=F32)
        z[j : j + step, 8 : 8 + cols] = got.reshape(step, cols, 5 * chans)
    got = lax.dot_general(rim[...].reshape(4 * LONG, hid), weights, NT, preferred_element_type=F32)
    for k, s in enumerate((7, 8, 7 + cols, 8 + cols)):
        for j in range(rows + 2):
            z[j, s : s + 1] = got[k * LONG + j : k * LONG + j + 1]
    cut = lambda j, t, s: z[j, 8 + s : 8 + s + cols, t * chans : (t + 1) * chans]
    for r in range(rows):
        j = r + 1
        total = cut(j, 0, 0) + cut(j - 1, 2, 0) + cut(j + 1, 2, 0)
        total += cut(j, 1, 1) + cut(j + 1, 3, 1) + cut(j - 1, 4, 1)
        total += cut(j, 1, -1) + cut(j - 1, 3, -1) + cut(j + 1, 4, -1)
        total += pack[:, OUT_AT : OUT_AT + chans] + cells[r].astype(F32)
        flat[pl.ds(r, chans, stride=rows), :] = total.T
    new_state[...] = flat[...].reshape(chans, rows, cols).astype(BF16)
    done[...] = jnp.zeros_like(done)


def out_part(hidden, rim, cells, conv_out, pack):
    rows, cols, chans = cells.shape
    return call(
        out_kernel,
        [jax.ShapeDtypeStruct((chans, rows, cols), BF16), jax.ShapeDtypeStruct((8, cols), F32)],
        [((rows + 2, cols + 16, 5 * chans), F32), ((chans * rows, cols), F32)],
        (2 * 18 * 128 * 640 * 256, 3000000, 0),
        18,
        *hidden, rim, cells, conv_out, pack,
    )


def sort_kernel(place, held, done, sent):
    count, chans, rows, cols = held.shape
    named = [place[k] for k in range(count)]
    chosen = [[v == p for v in named] for p in range(sent.shape[0])]
    for o in range(chans):
        for i in range(0, rows, 16):
            parts = [held[k, o, i : i + 16].astype(F32) for k in range(count)]
            parts = [(v[:8], v[8:]) for v in parts]
            for p in range(sent.shape[0]):
                total = [jnp.zeros((8, cols), F32)] * 2
                for k, v in enumerate(parts):
                    total = [jnp.where(chosen[p][k], x, t) for x, t in zip(v, total)]
                sent[p, o, i : i + 16] = jnp.concatenate(total).astype(BF16)


def sort_tiles(place, held, done, count):
    shape = jax.ShapeDtypeStruct((count,) + held.shape[1:], BF16)
    return call(sort_kernel, shape, [], (100000, 6 * held.size, 0), 6, place, held, done)


def exchange(values, partner):
    shape = tuple(lax.axis_size(a) for a in ALL)
    number = lambda f, r, c: (f * shape[1] + r) * shape[2] + c
    pairs = []
    for f in range(shape[0]):
        for r in range(shape[1]):
            for c in range(shape[2]):
                other = partner(f, r, c, shape)
                if other is not None:
                    pairs.append((number(f, r, c), number(*other)))
    return lax.ppermute(values, ALL, pairs)


def col_near(f, r, c, shape):
    return (f, r, c ^ 1)


def col_far(f, r, c, shape):
    if c == 0:
        return (f ^ 2, shape[1] - 1 - r, c)
    if c == shape[2] - 1:
        return (f ^ 1, shape[1] - 1 - r, c)
    return (f, r, ((c + 1) ^ 1) - 1)


def row_near(f, r, c, shape):
    return (f, r ^ 1, c)


def row_far(f, r, c, shape):
    return None if r in (0, shape[1] - 1) else (f, ((r + 1) ^ 1) - 1, c)


def local(state, conv_in, bias_in, conv_out, bias_out, land, owner):
    state = state[0]
    chans, height, width = state.shape
    rows, cols = lax.axis_size("row"), lax.axis_size("col")
    r, c = lax.axis_index("row"), lax.axis_index("col")
    lines = (r > 0, r < rows - 1, r, c, cols - 1, 0, 0, 0)
    here = jnp.concatenate([jnp.full((1, 128), v, jnp.int32) for v in lines])
    cells, edges, far, near, first = turn(here, state)

    far_rows, near_rows = exchange(far, row_far), exchange(near, row_near)

    tall, far, near = strips(here, edges, far_rows, near_rows)
    got_far = exchange(far, col_far)
    got_near = exchange(near, col_near)
    odd = c % 2 == 1
    got_near = jnp.concatenate([jnp.where(odd, got_near, 0), jnp.where(odd, 0, got_near)])

    lane = lambda v: jnp.pad(v.astype(F32), ((0, 0), (0, 128 - v.shape[1])))
    pack = jnp.concatenate([lane(owner), lane(land), bias_in[None], bias_out[None]], axis=1)
    target, place = routes(pack, here)
    cells = cells.astype(BF16)
    *hidden, sea = inner_part(here, cells, far_rows, near_rows, conv_in, pack, conv_out, first)
    rim, blocks = rim_part(here, target, tall, got_far, got_near, conv_in, pack, conv_out, sea, rows, OC)
    held = lax.all_to_all(blocks, "row", 0, 0, tiled=True)
    new_state, done = out_part(hidden, rim, cells, conv_out, pack)
    sent = sort_tiles(place, held, done, cols * CAP).reshape((cols, CAP, OC, height, width))
    got = lax.all_to_all(sent, "col", 0, 0, tiled=True)
    ocean = jnp.sum(got.astype(F32), axis=0).astype(BF16)
    return (new_state[None], ocean[None, None])


def solution(mesh):
    in_specs = (P("face", None, "row", "col"), P(), P(), P(), P(), P("face", None), P("face", None))
    out_specs = (P("face", None, "row", "col"), P("face", ("row", "col"), None, None, None, None))
    return jax.shard_map(local, mesh=mesh, in_specs=in_specs, out_specs=out_specs, check_vma=False)
```
